32 devices in a mesh: dp: 4 (over y, core), ctx: 8 (over z, x).
Axes of the slice: x: 2, y: 2, z: 4, core: 2. Of those that a mesh axis runs over, the one named last changes fastest.
Arguments:
- tokens: bfloat16 [4096, 768], P(('dp', 'ctx')), may hold values from -6 to 6
- w_qkv: bfloat16 [768, 2304], P('dp'), may hold values from -0.21875 to 0.21875
- w_attn_out: bfloat16 [768, 768], P('dp'), may hold values from -6 to 6
- w_in: bfloat16 [768, 2304], P('dp'), may hold values from -0.21875 to 0.21875
- w_down: bfloat16 [1152, 768], P('dp'), may hold values from -0.1875 to 0.1875
- gain_attn: bfloat16 [768], P('dp'), may hold values from 0.25 to 1.75
- gain_mlp: bfloat16 [768], P('dp'), may hold values from 0.25 to 1.75
- cotangent: bfloat16 [4096, 768], P(('dp', 'ctx')), may hold values from -6 to 6
Outputs:
- layer_out: bfloat16 [4096, 768], P(('dp', 'ctx'))
- tokens_grad: float32 [4096, 768], P(('dp', 'ctx'))
- w_qkv_grad: float32 [768, 2304], P('dp')
- w_attn_out_grad: float32 [768, 768], P('dp')
- w_in_grad: float32 [768, 2304], P('dp')
- w_down_grad: float32 [1152, 768], P('dp')
- gain_attn_grad: float32 [768], P('dp')
- gain_mlp_grad: float32 [768], P('dp')
The draws below stay inside these ranges and needn't reach their ends.
All inputs are finite; a program needn't handle non-finite values.
Results may differ from the reference program's by a relative error of at most 0.02.
Values may be sent and summed in bfloat16 or wider, within the bound.
No kernel may reach another device: no remote copies, remote signals or barrier semaphores. Data moves between devices by JAX's collectives and lax.ppermute only.
A program may use at most 192 MiB of HBM per device.

```python
import math
import jax
import jax.numpy as jnp
from jax import lax

D = 768
HEADS = 12
HEAD_DIM = 64
FF = 1152
SEQ_LEN = 1024
TOKENS = 4096
N_DP = 4


def steps_of(own_key, dims, pieces, smallest, high):
    loudness = 1.0
    for dim, blocks in pieces:
        draws = jax.random.uniform(jax.random.fold_in(jax.random.fold_in(own_key, 6), dim), (blocks,), jnp.float32, smallest / len(pieces), high / len(pieces))
        loudness = loudness * jnp.repeat(jnp.exp(draws), dims[dim] // blocks).reshape((-1,) + (1,) * (len(dims) - 1 - dim))
    return loudness


def bell_draw(rng, extent, width, limit, cuts=(), kind=jnp.bfloat16):
    array = width * jax.random.normal(rng, extent, jnp.float32)
    if cuts:
        array = array * steps_of(rng, extent, cuts, -0.22, 0.18)
    return jnp.clip(array, -limit, limit).astype(kind)


def setup_inputs(seed: int = 0) -> dict:
    keys = jax.random.split(jax.random.key(seed), 9)
    return {
        "tokens": bell_draw(keys[0], (TOKENS, D), 1.0, 6.0, ((0, 32),)),
        "w_qkv": bell_draw(keys[1], (D, 3 * D), D ** -0.5, 0.21875, ((0, 4),)),
        "w_attn_out": bell_draw(keys[2], (D, D), 1 ** -0.5, 6.0, ((0, 4),)),
        "w_in": bell_draw(keys[3], (D, 2 * FF), D ** -0.5, 0.21875, ((0, 4),)),
        "w_down": bell_draw(keys[4], (FF, D), FF ** -0.5, 0.1875, ((0, 4),)),
        "gain_attn": jnp.clip(1.0 + 0.15 * jax.random.normal(keys[5], (D,), jnp.float32), 0.25, 1.75).astype(jnp.bfloat16),
        "gain_mlp": jnp.clip(1.0 + 0.15 * jax.random.normal(keys[6], (D,), jnp.float32), 0.25, 1.75).astype(jnp.bfloat16),
        "cotangent": bell_draw(keys[7], (TOKENS, D), 1.0, 6.0, ((0, 32),)),
    }


theta_base = 160000.0
norm_eps = 1e-05

@jax.custom_vjp
def low(v):
    return lax.optimization_barrier(v.astype(jnp.bfloat16)).astype(jnp.float32)

@jax.custom_vjp
def low_back(v):
    return v

def low_keep(v):
    return (low(v), None)

def low_pass(kept, grad):
    return (grad,)

def back_keep(v):
    return (v, None)

def back_low(kept, grad):
    return (low(grad),)
low.defvjp(low_keep, low_pass)
low_back.defvjp(back_keep, back_low)

def layer_norm(values, gain):
    center = values - lax.optimization_barrier(jnp.mean(values, axis=-1, keepdims=True))
    spread = lax.optimization_barrier(jnp.mean(center * center, axis=-1, keepdims=True))
    return center * lax.rsqrt(spread + norm_eps) * gain

def rope_tables(positions, head_size):
    half_size = head_size // 2
    frequencies = jnp.exp(jnp.arange(half_size, dtype=jnp.float32) * (-2.0 * math.log(theta_base) / head_size))
    angles = positions[:, None] * frequencies[None, :]
    return (jnp.cos(angles), jnp.sin(angles))

def rotate(values, cosine_table, sine_table):
    half_size = values.shape[-1] // 2
    first_half = values[..., :half_size]
    second_half = values[..., half_size:]
    cos_part = cosine_table[:, None, :]
    sin_part = sine_table[:, None, :]
    return jnp.concatenate([first_half * cos_part - second_half * sin_part, second_half * cos_part + first_half * sin_part], axis=-1)

def matmul(left, right):
    return jnp.dot(left, right, precision=lax.Precision.HIGHEST, preferred_element_type=jnp.float32)

def attend_sequence(seq_parts, cosine_table, sine_table):
    queries_low = low(rotate(seq_parts[:, 0], cosine_table, sine_table))
    keys_low = low(rotate(seq_parts[:, 1], cosine_table, sine_table))
    values_low = low(seq_parts[:, 2])
    block_rows = math.gcd(SEQ_LEN, 512)
    score_scale = HEAD_DIM ** (-0.5)

    @jax.checkpoint
    def attend_block(query_block):
        scores = jnp.einsum('qhd,khd->hqk', query_block, keys_low, precision=lax.Precision.HIGHEST) * score_scale
        scores = low_back(scores)
        highest = lax.optimization_barrier(jnp.max(scores, axis=-1, keepdims=True))
        weights = jnp.exp(scores - highest)
        probs = low(weights / lax.optimization_barrier(jnp.sum(weights, axis=-1, keepdims=True)))
        return jnp.einsum('hqk,khd->qhd', probs, values_low, precision=lax.Precision.HIGHEST)
    blocks = queries_low.reshape(SEQ_LEN // block_rows, block_rows, HEADS, HEAD_DIM)
    return lax.map(attend_block, blocks).reshape(SEQ_LEN, HEADS * HEAD_DIM)

def forward(tokens, w_qkv, w_attn_out, w_in, w_down, gain_attn, gain_mlp):
    normed = low(layer_norm(tokens, gain_attn))
    projected = low_back(matmul(normed, w_qkv))
    parts = projected.reshape(N_DP, SEQ_LEN, 3, HEADS, HEAD_DIM)
    positions = jnp.arange(SEQ_LEN, dtype=jnp.int32).astype(jnp.float32)
    cosine_table, sine_table = rope_tables(positions, HEAD_DIM)

    def one_sequence(seq_parts):
        return attend_sequence(seq_parts, cosine_table, sine_table)
    attn = lax.map(one_sequence, parts).reshape(TOKENS, D)
    attn_low = low(low_back(attn))
    branch = low_back(matmul(attn_low, w_attn_out))
    middle = tokens + branch
    normed_two = low(layer_norm(middle, gain_mlp))
    up_proj = low_back(matmul(normed_two, w_in))
    hidden = low(jax.nn.gelu(up_proj[:, :FF], approximate=False) * up_proj[:, FF:])
    return middle + matmul(hidden, w_down)

def reference(tokens, w_qkv, w_attn_out, w_in, w_down, gain_attn, gain_mlp, cotangent):
    result, backward = jax.vjp(forward, tokens.astype(jnp.float32), w_qkv.astype(jnp.float32), w_attn_out.astype(jnp.float32), w_in.astype(jnp.float32), w_down.astype(jnp.float32), gain_attn.astype(jnp.float32), gain_mlp.astype(jnp.float32))
    grads = backward(cotangent.astype(jnp.float32))
    return (result.astype(jnp.bfloat16), grads[0], grads[1], grads[2], grads[3], grads[4], grads[5], grads[6])
```

```python
import functools
import math

import jax
import jax.numpy as jnp
import numpy as np
from jax import lax
from jax.experimental import pallas as pl
from jax.experimental.pallas import tpu as pltpu
from jax.sharding import PartitionSpec as P

HEADS = 12
HEAD_DIM = 64
THETA = 160000.0
EPS = 1e-05
CHUNK_BITS = 3
CHUNKS = 1 << CHUNK_BITS
BF = jnp.bfloat16
F32 = jnp.float32
VMEM_LIMIT = 58 * 1024 * 1024


def whole(shape):
    return pl.BlockSpec(shape, lambda *_: (0,) * len(shape))


def params(limit=VMEM_LIMIT):
    return pltpu.CompilerParams(vmem_limit_bytes=limit)


def cost(flops, moved, trans=0):
    return pl.CostEstimate(flops=int(flops), bytes_accessed=int(moved), transcendentals=int(trans))


def dot(left, right, dims=((1,), (0,))):
    return lax.dot_general(left, right, (dims, ((), ())), preferred_element_type=F32)


NT = ((1,), (1,))
TN = ((0,), (0,))


def normalise(values):
    center = values - jnp.mean(values, axis=-1, keepdims=True)
    spread = jnp.mean(center * center, axis=-1, keepdims=True)
    scale = lax.rsqrt(spread + EPS)
    return center * scale, scale


def norm_back(grad, xhat, scale, gain):
    inner = grad * gain
    return scale * (
        inner
        - jnp.mean(inner, axis=-1, keepdims=True)
        - xhat * jnp.mean(inner * xhat, axis=-1, keepdims=True)
    )


def swap_halves(values):
    lane = lax.broadcasted_iota(jnp.int32, values.shape, 1)
    return jnp.where(lane % 64 < 32, pltpu.roll(values, 96, 1), pltpu.roll(values, 32, 1))


def rotate(values, cos, sin):
    return values * cos + swap_halves(values) * sin


def rotate_back(values, cos, sin):
    return values * cos - swap_halves(values) * sin


def fold(pieces):
    rows = [p[8 * i : 8 * i + 8] for p in pieces for i in range(p.shape[0] // 8)]
    flat = jnp.concatenate(rows, axis=1)
    half = flat.shape[1] // 2
    return jnp.concatenate([flat[:, :half], flat[:, half:]], axis=0)


def unfold(block, shapes):
    flat = jnp.concatenate([block[:8], block[8:]], axis=1)
    out, at = [], 0
    for rows, cols in shapes:
        parts = []
        for _ in range(rows // 8):
            parts.append(flat[:, at : at + cols])
            at += cols
        out.append(jnp.concatenate(parts, axis=0))
    return out


def place(svec, j, chunk):
    keep = j & 1
    upper = j >> 1
    core = (svec[0] & 1) ^ keep
    rel = chunk ^ svec[1 + keep]
    low = CHUNK_BITS - 1
    first = upper * CHUNKS + rel
    second = ((rel >> low) << CHUNK_BITS) | (upper << low) | (rel & ((1 << low) - 1))
    return jnp.where(core == 0, first, second)


def qkv_kernel(svec, x_ref, w0, w1, w2, w3, gain_ref, cos_ref, sin_ref, n_ref, q_ref, k_ref, v_ref, w_ref, *, own):
    rows = w_ref.shape[0] // 4
    width = n_ref.shape[1]

    @pl.when(pl.program_id(0) == 0)
    def _():
        for j, piece in enumerate((w0, w1, w2, w3)):
            at = pl.multiple_of((svec[0] ^ j) * rows, 16)
            w_ref[pl.ds(at, rows), :] = piece[:rows, :]

    xhat, _ = normalise(x_ref[...].astype(F32))
    normed = (xhat * gain_ref[...]).astype(BF)
    n_ref[...] = normed
    cos, sin = cos_ref[...], sin_ref[...]
    keys = dot(normed, w_ref[:, width : 2 * width])
    for g in range(width // 128):
        cut = slice(128 * g, 128 * g + 128)
        k_ref[:, cut] = rotate(keys[:, cut], cos, sin).astype(BF)
    v_ref[...] = dot(normed, w_ref[:, 2 * width :]).astype(BF)

    @pl.when(pl.program_id(0) == 0)
    def _():
        queries = dot(normed[:own], w_ref[:, :width])
        for g in range(width // 128):
            cut = slice(128 * g, 128 * g + 128)
            q_ref[:, cut] = rotate(queries[:, cut], cos[:own], sin[:own]).astype(BF)


def head_mask(shape, head):
    return lax.broadcasted_iota(jnp.int32, shape, 1) // HEAD_DIM == head


def fold_scale(q, head):
    return jnp.where(head_mask(q.shape, head), q, jnp.zeros_like(q)) * jnp.asarray(HEAD_DIM**-0.5, BF)


def attend_kernel(q_ref, k_ref, v_ref, o_ref, lse_ref):
    q, k, v = q_ref[...], k_ref[...], v_ref[...]
    for h in range(2):
        scores = dot(k, fold_scale(q, h), NT)
        top = jnp.max(scores, axis=0, keepdims=True)
        weights = jnp.exp(scores - top)
        total = jnp.sum(weights, axis=0, keepdims=True)
        out = dot(v, weights.astype(BF), TN)
        cut = slice(HEAD_DIM * h, HEAD_DIM * h + HEAD_DIM)
        o_ref[cut, :] = out[cut, :] / total
        lse_ref[0, h : h + 1, :] = top + jnp.log(total)


def middle_kernel(
    svec, x_ref, at_ref, p0, p1, p2, p3, dy_ref, gain_ref,
    lo_ref, dm_ref, da_ref, dat_ref, gk_ref, gs_ref,
    win, wout, wdown, n2t, attnt, hidt,
):
    width = x_ref.shape[1]
    rows = width // 4
    ff = wdown.shape[0]
    frows = ff // 4
    for j, piece in enumerate((p0, p1, p2, p3)):
        at = pl.multiple_of((svec[0] ^ j) * rows, 16)
        for b in range(3):
            win[pl.ds(at, rows), b * width : (b + 1) * width] = piece[b * rows : (b + 1) * rows, :]
        wout[pl.ds(at, rows), :] = piece[3 * rows : 4 * rows, :]
        fat = pl.multiple_of((svec[0] ^ j) * frows, 16)
        wdown[pl.ds(fat, frows), :] = piece[4 * rows : 4 * rows + frows, :]

    gain = gain_ref[...]
    attn_t = at_ref[...]
    attnt[...] = attn_t.astype(BF)
    attn_low = jnp.transpose(attn_t).astype(BF)
    mid = x_ref[...].astype(F32) + dot(attn_low, wout[...])
    xhat, scale = normalise(mid)
    normed = xhat * gain
    n2t[...] = jnp.transpose(normed).astype(BF)
    up = dot(normed.astype(BF), win[...])
    gate, lin = up[:, :ff], up[:, ff:]
    cdf = 0.5 * (1.0 + lax.erf(gate * (2.0**-0.5)))
    act = gate * cdf
    hidden = act * lin
    hidt[...] = jnp.transpose(hidden).astype(BF)
    lo_ref[...] = (mid + dot(hidden.astype(BF), wdown[...])).astype(BF)
    dy = dy_ref[...]
    d_hidden = dot(dy, wdown[...], NT)
    pdf = jnp.exp(-0.5 * gate * gate) * (1.0 / math.sqrt(2.0 * math.pi))
    d_gate = (d_hidden * lin * (cdf + gate * pdf)).astype(BF)
    d_lin = (d_hidden * act).astype(BF)
    d_up = jnp.concatenate([d_gate, d_lin], axis=1)
    d_mid = dy.astype(F32) + norm_back(dot(d_up, win[...], NT), xhat, scale, gain)
    dm_ref[...] = d_mid
    d_branch = d_mid.astype(BF)
    da_ref[...] = dot(d_branch, wout[...], NT).astype(BF)
    dat_ref[...] = dot(wout[...], d_branch, NT).astype(BF)
    for j in (1, 3, 2, 0):
        q = svec[0] ^ j
        at = pl.multiple_of(q * rows, 16)
        fat = pl.multiple_of(q * frows, 16)
        g_in = dot(n2t[pl.ds(at, rows), :], d_up)
        g_out = dot(attnt[pl.ds(at, rows), :], d_branch)
        g_down = dot(hidt[pl.ds(fat, frows), :], dy)
        target = gs_ref if j & 1 else gk_ref
        step = rows // CHUNKS
        fstep = frows // CHUNKS
        for c in range(CHUNKS):
            fs = 2 * fstep * (c // 2) + (fstep - 4) * (c % 2)
            block = fold(
                [g_in[c * step : (c + 1) * step], g_out[c * step : (c + 1) * step], g_down[fs : fs + fstep + 4]]
            )
            target[place(svec, j, c)] = block.astype(BF)


def attend_back_kernel(q_ref, k_ref, v_ref, da_ref, dat_ref, at_ref, lse_ref, cos_ref, sin_ref, dq_ref, dkv_ref):
    q, k, v, da = q_ref[...], k_ref[...], v_ref[...], da_ref[...]
    own = q.shape[0]
    prod = dat_ref[...].astype(F32) * at_ref[...]
    d_key, d_value, d_query = 0.0, 0.0, []
    for h in range(2):
        cut = slice(HEAD_DIM * h, HEAD_DIM * h + HEAD_DIM)
        q_scaled = fold_scale(q, h)
        da_head = jnp.where(head_mask(da.shape, h), da, jnp.zeros_like(da))
        probs = jnp.exp(dot(k, q_scaled, NT) - lse_ref[0, h : h + 1, :])
        delta = jnp.sum(prod[cut, :], axis=0, keepdims=True)
        d_scores = (probs * (dot(v, da_head, NT) - delta)).astype(BF)
        d_value += dot(probs.astype(BF), da_head)
        d_key += dot(d_scores, q_scaled)
        d_query.append(dot(d_scores, k, TN))
    dkv_ref[0] = rotate_back(d_key, cos_ref[...], sin_ref[...]).astype(BF)
    dkv_ref[1] = d_value.astype(BF)
    d_q = jnp.where(head_mask(q.shape, 0), d_query[0], d_query[1]) * (HEAD_DIM**-0.5)
    dq_ref[...] = rotate_back(d_q, cos_ref[:own, :], sin_ref[:own, :]).astype(BF)


def qkv_grad_kernel(svec, n_ref, dkv_ref, dq_ref, gk_ref, gs_ref, acc):
    width = n_ref.shape[1]
    rows = width // 4
    step = rows // CHUNKS
    own = dq_ref.shape[0]
    normed = n_ref[...]
    first = pl.program_id(0) == 0

    @pl.when(first)
    def _():
        acc[:, :width] = dot(normed[:own], dq_ref[...], TN)
        for b in range(2):
            acc[:, (b + 1) * width : (b + 2) * width] = dot(normed, dkv_ref[b], TN)

    @pl.when(jnp.logical_not(first))
    def _():
        for b in range(2):
            acc[:, (b + 1) * width : (b + 2) * width] += dot(normed, dkv_ref[b], TN)

    @pl.when(pl.program_id(0) == pl.num_programs(0) - 1)
    def _():
        for j in (1, 3, 2, 0):
            target = gs_ref if j & 1 else gk_ref
            at = pl.multiple_of((svec[0] ^ j) * rows, 8)
            for c in range(CHUNKS):
                block = acc[pl.ds(pl.multiple_of(at + c * step, 8), step), :]
                target[place(svec, j, c)] = fold([block]).astype(BF)


def tokens_grad_kernel(x_ref, dq_ref, dkv_ref, w_ref, gain_ref, dm_ref, out_ref):
    d_proj = jnp.concatenate([dq_ref[...], dkv_ref[0], dkv_ref[1]], axis=1)
    d_normed = dot(d_proj, w_ref[...], NT)
    xhat, scale = normalise(x_ref[...].astype(F32))
    out_ref[...] = dm_ref[...] + norm_back(d_normed, xhat, scale, gain_ref[...])


def finish_first_kernel(svec, ra, rb, w_ref, in_ref, out_ref, down_ref, gain_ref, *, step, fstep, width):
    shapes = ((step, 3 * width), (step, width), (fstep + 4, width))
    parts_a = unfold(ra[0].astype(F32), shapes)
    parts_b = unfold(rb[0].astype(F32), shapes)
    both = [jnp.concatenate([a, b], axis=0) for a, b in zip(parts_a[:2], parts_b[:2])]
    in_ref[...] = both[0]
    out_ref[...] = both[1]
    down_ref[...] = jnp.concatenate([parts_a[2], parts_b[2][8:]], axis=0)
    total = jnp.sum(w_ref[...].astype(F32) * both[0], axis=1, keepdims=True)
    gain_ref[...] = jnp.broadcast_to(total, gain_ref.shape)


def finish_second_kernel(svec, ra, rb, w_ref, out_ref, gain_ref, *, step, width):
    shapes = ((step, 3 * width),)
    grad = jnp.concatenate([unfold(ra[0].astype(F32), shapes)[0], unfold(rb[0].astype(F32), shapes)[0]], axis=0)
    out_ref[...] = grad
    total = jnp.sum(w_ref[...].astype(F32) * grad, axis=1, keepdims=True)
    gain_ref[...] = jnp.broadcast_to(total, gain_ref.shape)


class Links:
    def __init__(self, n_dp, n_ctx):
        self.n_dp, self.n_ctx = n_dp, n_ctx
        self.bits = n_ctx.bit_length() - 1
        rise = list(range(self.bits))
        self.orders = (rise, rise[1:] + rise[:1])

    def swap(self, value, dims):
        pairs = []
        for d in range(self.n_dp):
            dim = dims[d & 1]
            for c in range(self.n_ctx):
                if dim == "core":
                    to = (d ^ 1, c)
                elif dim == "y":
                    to = (d ^ 2, c)
                else:
                    to = (d, c ^ (1 << dim))
                pairs.append((d * self.n_ctx + c, to[0] * self.n_ctx + to[1]))
        return lax.ppermute(value, ("dp", "ctx"), pairs)

    def both(self, step):
        return (self.orders[0][step], self.orders[1][step])


def add_low(left, right):
    return (left.astype(F32) + right.astype(F32)).astype(BF)


def reduce_chunks(links, keep, send):
    recv = links.swap(send, ("core", "core"))
    walk = [list(o[:CHUNK_BITS]) for o in links.orders]
    walk[0].insert(0, "y")
    walk[1].insert(1, "y")
    for step in range(CHUNK_BITS + 1):
        half = keep.shape[0] // 2
        send = add_low(keep[half:], recv[half:])
        keep = add_low(keep[:half], recv[:half])
        recv = links.swap(send, (walk[0][step], walk[1][step]))
    total = add_low(keep, recv)
    for step in range(CHUNK_BITS, links.bits):
        total = add_low(total, links.swap(total, links.both(step)))
    for step in reversed(range(CHUNK_BITS)):
        total = jnp.concatenate([total, links.swap(total, links.both(step))], axis=0)
    return total


def on_device(tokens, w_qkv, w_attn_out, w_in, w_down, gain_attn, gain_mlp, cotangent, *, n_dp, n_ctx):
    links = Links(n_dp, n_ctx)
    own, width = tokens.shape
    rows = w_qkv.shape[0]
    frows = w_down.shape[0]
    ff = frows * n_dp
    seq = own * n_ctx
    groups = width // 128
    step, fstep = rows // CHUNKS, frows // CHUNKS
    dp_at = lax.axis_index("dp")
    ctx_at = lax.axis_index("ctx")
    core = dp_at & 1
    upper = dp_at >> 1

    marks = []
    for order in links.orders:
        mark = 0
        for i in range(CHUNK_BITS):
            mark = mark | (((ctx_at >> order[i]) & 1) << (CHUNK_BITS - 1 - i))
        marks.append(mark)
    mine = jnp.where(core == 0, marks[0], marks[1])
    other = jnp.where(core == 0, marks[1], marks[0])
    svec = jnp.stack([dp_at, mine, other]).astype(jnp.int32)

    gains_row = jnp.zeros((16, 3 * width), BF)
    gains_row = gains_row.at[0, :rows].set(gain_attn).at[1, :rows].set(gain_mlp)
    pack_qkv = jnp.concatenate([w_qkv, gains_row], axis=0)
    pack_rest = jnp.concatenate(
        [w_in[:, :width], w_in[:, width : 2 * width], w_in[:, 2 * width :], w_attn_out, w_down], axis=0
    )
    qkv_y = links.swap(pack_qkv, ("y", "y"))
    qkv_c = links.swap(pack_qkv, ("core", "core"))

    everyone = tokens
    for i in reversed(range(links.bits)):
        everyone = jnp.concatenate([everyone, links.swap(everyone, links.both(i))], axis=0)

    qkv_cy = links.swap(qkv_y, ("core", "core"))
    pack_late, _ = lax.optimization_barrier((pack_rest, qkv_y))
    rest_y = links.swap(pack_late, ("y", "y"))
    rest_c = links.swap(pack_late, ("core", "core"))
    rest_cy = links.swap(rest_y, ("core", "core"))

    def gain_of(row):
        g = [p[rows + row, :rows].astype(F32) for p in (pack_qkv, qkv_c, qkv_y, qkv_cy)]
        near = jnp.where(core == 0, jnp.concatenate([g[0], g[1]]), jnp.concatenate([g[1], g[0]]))
        far = jnp.where(core == 0, jnp.concatenate([g[2], g[3]]), jnp.concatenate([g[3], g[2]]))
        full = jnp.where(upper == 0, jnp.concatenate([near, far]), jnp.concatenate([far, near]))
        return full.reshape(1, width)

    gain_one, gain_two = gain_of(0), gain_of(1)

    flips = []
    for order in links.orders:
        at = np.arange(n_ctx)
        flips.append(sum(((at >> i) & 1) << order[links.bits - 1 - i] for i in range(links.bits)).astype(np.int32))
    owner = ctx_at ^ jnp.where(core == 0, jnp.asarray(flips[0]), jnp.asarray(flips[1]))
    positions = (owner[:, None] * own + jnp.arange(own, dtype=jnp.int32)[None, :]).reshape(seq).astype(F32)
    half = HEAD_DIM // 2
    frequencies = jnp.exp(jnp.arange(half, dtype=F32) * (-2.0 * math.log(THETA) / HEAD_DIM))
    angles = positions[:, None] * frequencies[None, :]
    cos, sin = jnp.cos(angles), jnp.sin(angles)
    cos = jnp.concatenate([cos] * 4, axis=1)
    sin = jnp.concatenate([-sin, sin, -sin, sin], axis=1)

    block = math.gcd(seq, 256)
    normed, queries, keys, values, full_qkv = pl.pallas_call(
        functools.partial(qkv_kernel, own=own),
        grid_spec=pltpu.PrefetchScalarGridSpec(
            num_scalar_prefetch=1,
            grid=(seq // block,),
            in_specs=[pl.BlockSpec((block, width), lambda i, s: (i, 0))]
            + [whole(pack_qkv.shape)] * 4
            + [whole((1, width))]
            + [pl.BlockSpec((block, 128), lambda i, s: (i, 0))] * 2,
            out_specs=[
                pl.BlockSpec((block, width), lambda i, s: (i, 0)),
                whole((own, width)),
                pl.BlockSpec((block, width), lambda i, s: (i, 0)),
                pl.BlockSpec((block, width), lambda i, s: (i, 0)),
                whole((width, 3 * width)),
            ],
        ),
        out_shape=[
            jax.ShapeDtypeStruct((seq, width), BF),
            jax.ShapeDtypeStruct((own, width), BF),
            jax.ShapeDtypeStruct((seq, width), BF),
            jax.ShapeDtypeStruct((seq, width), BF),
            jax.ShapeDtypeStruct((width, 3 * width), BF),
        ],
        compiler_params=params(),
        cost_estimate=cost(4 * seq * width * width, 14e6),
        name="qkv",
    )(svec, everyone, pack_qkv, qkv_c, qkv_y, qkv_cy, gain_one, cos, sin)

    own_pair = pl.BlockSpec((own, 128), lambda g: (0, g))
    seq_pair = pl.BlockSpec((seq, 128), lambda g: (0, g))
    turned_pair = pl.BlockSpec((128, own), lambda g: (g, 0))
    lse_pair = pl.BlockSpec((1, 8, own), lambda g: (g, 0, 0))
    attn_t, lse = pl.pallas_call(
        attend_kernel,
        grid=(groups,),
        in_specs=[own_pair, seq_pair, seq_pair],
        out_specs=[turned_pair, lse_pair],
        out_shape=[jax.ShapeDtypeStruct((width, own), F32), jax.ShapeDtypeStruct((groups, 8, own), F32)],
        compiler_params=params(),
        cost_estimate=cost(8 * seq * own * width, 4e6, seq * own * HEADS),
        name="attend",
    )(queries, keys, values)

    vm = pl.BlockSpec(memory_space=pltpu.VMEM)
    length = (3 * step * 4 * width // 3 + (fstep + 4) * width) // 16
    layer_out, d_mid, d_attn, d_attn_t, first_keep, first_send = pl.pallas_call(
        middle_kernel,
        in_specs=[pl.BlockSpec(memory_space=pltpu.SMEM)] + [vm] * 8,
        out_specs=[vm] * 6,
        out_shape=[
            jax.ShapeDtypeStruct((own, width), BF),
            jax.ShapeDtypeStruct((own, width), F32),
            jax.ShapeDtypeStruct((own, width), BF),
            jax.ShapeDtypeStruct((width, own), BF),
            jax.ShapeDtypeStruct((2 * CHUNKS, 16, length), BF),
            jax.ShapeDtypeStruct((2 * CHUNKS, 16, length), BF),
        ],
        scratch_shapes=[
            pltpu.VMEM((width, 3 * width), BF),
            pltpu.VMEM((width, width), BF),
            pltpu.VMEM((ff, width), BF),
            pltpu.VMEM((width, own), BF),
            pltpu.VMEM((width, own), BF),
            pltpu.VMEM((ff, own), BF),
        ],
        compiler_params=params(),
        cost_estimate=cost(6 * own * width * (4 * width + ff), 16e6),
        name="middle",
    )(svec, tokens, attn_t, pack_rest, rest_c, rest_y, rest_cy, cotangent, gain_two)

    d_query, d_kv = pl.pallas_call(
        attend_back_kernel,
        grid=(groups,),
        in_specs=[
            own_pair, seq_pair, seq_pair, own_pair, turned_pair, turned_pair, lse_pair,
            whole((seq, 128)), whole((seq, 128)),
        ],
        out_specs=[own_pair, pl.BlockSpec((2, seq, 128), lambda g: (0, 0, g))],
        out_shape=[jax.ShapeDtypeStruct((own, width), BF), jax.ShapeDtypeStruct((2, seq, width), BF)],
        compiler_params=params(),
        cost_estimate=cost(20 * seq * own * width, 8e6, seq * own * HEADS),
        name="attend_back",
    )(queries, keys, values, d_attn, d_attn_t, attn_t, lse, cos, sin)

    deep = math.gcd(seq, 1024)
    second_keep, second_send = pl.pallas_call(
        qkv_grad_kernel,
        grid_spec=pltpu.PrefetchScalarGridSpec(
            num_scalar_prefetch=1,
            grid=(seq // deep,),
            in_specs=[
                pl.BlockSpec((deep, width), lambda i, s: (i, 0)),
                pl.BlockSpec((2, deep, width), lambda i, s: (0, i, 0)),
                whole((own, width)),
            ],
            out_specs=[whole((2 * CHUNKS, 16, step * 3 * width // 16))] * 2,
            scratch_shapes=[pltpu.VMEM((width, 3 * width), F32)],
        ),
        out_shape=[jax.ShapeDtypeStruct((2 * CHUNKS, 16, step * 3 * width // 16), BF)] * 2,
        compiler_params=params(),
        cost_estimate=cost(4 * seq * width * width, 9e6),
        name="qkv_grad",
    )(svec, normed, d_kv, d_query)

    first = reduce_chunks(links, first_keep, first_send)
    second = reduce_chunks(links, second_keep, second_send)

    for i in range(links.bits):
        mid = d_kv.shape[1] // 2
        d_kv = add_low(d_kv[:, :mid], links.swap(d_kv[:, mid:], links.both(i)))

    tokens_grad = pl.pallas_call(
        tokens_grad_kernel,
        in_specs=[vm] * 6,
        out_specs=vm,
        out_shape=jax.ShapeDtypeStruct((own, width), F32),
        compiler_params=params(),
        cost_estimate=cost(6 * own * width * width, 5e6),
        name="tokens_grad",
    )(tokens, d_query, d_kv, full_qkv, gain_one, d_mid)

    def pair_specs(length):
        return [
            pl.BlockSpec((1, 16, length), lambda i, s: ((2 * i) ^ s[1], 0, 0)),
            pl.BlockSpec((1, 16, length), lambda i, s: ((2 * i + 1) ^ s[1], 0, 0)),
        ]

    def row_spec(count, cols):
        return pl.BlockSpec((count, cols), lambda i, s: (i, 0))

    in_grad, out_grad, down_grad, gain_mlp_sum = pl.pallas_call(
        functools.partial(finish_first_kernel, step=step, fstep=fstep, width=width),
        grid_spec=pltpu.PrefetchScalarGridSpec(
            num_scalar_prefetch=1,
            grid=(CHUNKS // 2,),
            in_specs=pair_specs(length) + [row_spec(2 * step, 3 * width)],
            out_specs=[
                row_spec(2 * step, 3 * width),
                row_spec(2 * step, width),
                row_spec(2 * fstep, width),
                row_spec(2 * step, 128),
            ],
        ),
        out_shape=[
            jax.ShapeDtypeStruct((rows, 3 * width), F32),
            jax.ShapeDtypeStruct((rows, width), F32),
            jax.ShapeDtypeStruct((frows, width), F32),
            jax.ShapeDtypeStruct((rows, 128), F32),
        ],
        compiler_params=params(),
        cost_estimate=cost(1e6, 6e6),
        name="finish_first",
    )(svec, first, first, w_in)

    qkv_grad, gain_attn_sum = pl.pallas_call(
        functools.partial(finish_second_kernel, step=step, width=width),
        grid_spec=pltpu.PrefetchScalarGridSpec(
            num_scalar_prefetch=1,
            grid=(CHUNKS // 2,),
            in_specs=pair_specs(step * 3 * width // 16) + [row_spec(2 * step, 3 * width)],
            out_specs=[row_spec(2 * step, 3 * width), row_spec(2 * step, 128)],
        ),
        out_shape=[jax.ShapeDtypeStruct((rows, 3 * width), F32), jax.ShapeDtypeStruct((rows, 128), F32)],
        compiler_params=params(),
        cost_estimate=cost(1e6, 4e6),
        name="finish_second",
    )(svec, second, second, w_qkv)

    return (
        layer_out,
        tokens_grad,
        qkv_grad,
        out_grad,
        in_grad,
        down_grad,
        gain_attn_sum[:, 0] / gain_attn.astype(F32),
        gain_mlp_sum[:, 0] / gain_mlp.astype(F32),
    )


def solution(mesh):
    return jax.shard_map(
        functools.partial(on_device, n_dp=mesh.shape["dp"], n_ctx=mesh.shape["ctx"]),
        mesh=mesh,
        in_specs=(
            P(("dp", "ctx"), None),
            P("dp", None),
            P("dp", None),
            P("dp", None),
            P("dp", None),
            P("dp"),
            P("dp"),
            P(("dp", "ctx"), None),
        ),
        out_specs=(
            P(("dp", "ctx"), None),
            P(("dp", "ctx"), None),
            P("dp", None),
            P("dp", None),
            P("dp", None),
            P("dp", None),
            P("dp"),
            P("dp"),
        ),
        check_vma=False,
    )
```

```python
import functools
import math

import jax
import jax.numpy as jnp
import numpy as np
from jax import lax
from jax.experimental import pallas as pl
from jax.experimental.pallas import tpu as pltpu
from jax.sharding import PartitionSpec as P

HEADS = 12
HEAD_DIM = 64
THETA = 160000.0
EPS = 1e-05
CHUNK_BITS = 3
CHUNKS = 1 << CHUNK_BITS
BF = jnp.bfloat16
F32 = jnp.float32
COSTS = {
    "pack_up": 0.5,
    "qkv_near": 0.5,
    "qkv_far": 0.5,
    "attend": 0.5,
    "middle": 0.5,
    "middle_grad": 0.5,
    "every_query": 0.5,
    "attend_back": 0.5,
    "qkv_grad": 0.5,
    "attend_keys": 0.5,
    "tokens_grad": 0.5,
    "finish_first": 0.5,
    "finish_second": 0.5,
}
FIRST_WALKS = ((0, 1, 2), (1, 0, 2))
SECOND_WALKS = (("y", 0, 1, 2), (1, "y", 0, 2))
VMEM_LIMIT = 58 * 1024 * 1024


def whole(shape):
    return pl.BlockSpec(shape, lambda *_: (0,) * len(shape))


def params(limit=VMEM_LIMIT):
    return pltpu.CompilerParams(vmem_limit_bytes=limit)


def cost(micros):
    return pl.CostEstimate(flops=int(micros * 1.15e9), bytes_accessed=0, transcendentals=0)


def dot(left, right, dims=((1,), (0,))):
    return lax.dot_general(left, right, (dims, ((), ())), preferred_element_type=F32)


NT = ((1,), (1,))
TN = ((0,), (0,))


def normalise(values):
    center = values - jnp.mean(values, axis=-1, keepdims=True)
    spread = jnp.mean(center * center, axis=-1, keepdims=True)
    scale = lax.rsqrt(spread + EPS)
    return center * scale, scale


def norm_back(grad, xhat, scale, gain):
    inner = grad * gain
    return scale * (
        inner
        - jnp.mean(inner, axis=-1, keepdims=True)
        - xhat * jnp.mean(inner * xhat, axis=-1, keepdims=True)
    )


def swap_halves(values):
    lane = lax.broadcasted_iota(jnp.int32, values.shape, 1)
    return jnp.where(lane % 64 < 32, pltpu.roll(values, 96, 1), pltpu.roll(values, 32, 1))


def rotate(values, cos, sin):
    return values * cos + swap_halves(values) * sin


def rotate_back(values, cos, sin):
    return values * cos - swap_halves(values) * sin


def fold(pieces):
    rows = [p[8 * i : 8 * i + 8] for p in pieces for i in range(p.shape[0] // 8)]
    flat = jnp.concatenate(rows, axis=1)
    half = flat.shape[1] // 2
    return jnp.concatenate([flat[:, :half], flat[:, half:]], axis=0)


def unfold(block, shapes):
    flat = jnp.concatenate([block[:8], block[8:]], axis=1)
    out, at = [], 0
    for rows, cols in shapes:
        parts = []
        for _ in range(rows // 8):
            parts.append(flat[:, at : at + cols])
            at += cols
        out.append(jnp.concatenate(parts, axis=0))
    return out


def chunk_at(svec, keep, spot):
    found = []
    for walk in SECOND_WALKS:
        low = CHUNK_BITS - walk.index("y")
        rel = ((spot >> (low + 1)) << low) | (spot & ((1 << low) - 1))
        found.append(((spot >> low) & 1, rel))
    core = (svec[0] & 1) ^ keep
    upper = jnp.where(core == 0, found[0][0], found[1][0])
    return upper, jnp.where(core == 0, found[0][1], found[1][1]) ^ svec[3 + keep]


def spread(svec, pieces, half, begins, to_ref, to_cols):
    for j, parts in enumerate(pieces):
        halved = len(parts) == 3
        for h in range(2):
            to = (svec[0] ^ j) * (2 * half) + (svec[1] ^ h if halved else h) * half
            at = begins[1] if halved else begins[0] + h * half
            part = parts[h if halved else 0]
            to_ref[pl.ds(pl.multiple_of(to, 16), half), to_cols] = part[at : at + half, parts[-1]]


def pack_up_kernel(svec, in_ref, w_ref, out_ref):
    half, width = w_ref.shape
    for b in range(3):
        out_ref[b * half : (b + 1) * half, :] = in_ref[:, b * width : (b + 1) * width]
    out_ref[3 * half :, :] = w_ref[...]


def project(x_ref, gain, cos_ref, sin_ref, w_ref, n_ref, k_ref, v_ref):
    width = n_ref.shape[1]
    xhat, _ = normalise(x_ref[...].astype(F32))
    normed = (xhat * gain).astype(BF)
    n_ref[...] = normed
    cos, sin = cos_ref[...], sin_ref[...]
    keys = dot(normed, w_ref[:, width : 2 * width])
    for g in range(width // 128):
        cut = slice(128 * g, 128 * g + 128)
        k_ref[:, cut] = rotate(keys[:, cut], cos, sin).astype(BF)
    v_ref[...] = dot(normed, w_ref[:, 2 * width :]).astype(BF)
    return normed, cos, sin


def qkv_near_kernel(
    svec, x_ref, w0, w1, w2, w3, g0_ref, g1_ref, g2_ref, g3_ref, cos_ref, sin_ref,
    n_ref, q_ref, k_ref, v_ref, w_ref, gain_ref, *, own,
):
    rows = w_ref.shape[0] // 4
    width = n_ref.shape[1]
    first = pl.program_id(0) == 0

    @pl.when(first)
    def _():
        for j, piece in enumerate((w0, w1, w2, w3)):
            w_ref[pl.ds(pl.multiple_of((svec[0] ^ j) * rows, 16), rows), :] = piece[...]
        g = [r[:, :rows] for r in (g0_ref, g1_ref, g2_ref, g3_ref)]
        core, upper = svec[0] & 1, svec[0] >> 1
        near = jnp.where(core == 0, jnp.concatenate([g[0], g[1]], axis=1), jnp.concatenate([g[1], g[0]], axis=1))
        far = jnp.where(core == 0, jnp.concatenate([g[2], g[3]], axis=1), jnp.concatenate([g[3], g[2]], axis=1))
        full = jnp.where(upper == 0, jnp.concatenate([near, far], axis=1), jnp.concatenate([far, near], axis=1))
        gain_ref[...] = full

    normed, cos, sin = project(x_ref, gain_ref[0:1, :], cos_ref, sin_ref, w_ref, n_ref, k_ref, v_ref)

    @pl.when(first)
    def _():
        queries = dot(normed[:own], w_ref[:, :width])
        for g in range(width // 128):
            cut = slice(128 * g, 128 * g + 128)
            q_ref[:, cut] = rotate(queries[:, cut], cos[:own], sin[:own]).astype(BF)


def qkv_far_kernel(x_ref, w_ref, gain_ref, cos_ref, sin_ref, n_ref, k_ref, v_ref):
    project(x_ref, gain_ref[0:1, :], cos_ref, sin_ref, w_ref, n_ref, k_ref, v_ref)


def both_halves(near_ref, far_ref):
    return jnp.concatenate([near_ref[...], far_ref[...]], axis=0)


def queries_kernel(near_ref, far_ref, w_ref, cos_ref, sin_ref, q_ref):
    there = pl.program_id(0) >= pl.num_programs(0) // 2
    queries = dot(jnp.where(there, far_ref[...], near_ref[...]), w_ref[...])
    cos, sin = cos_ref[...], sin_ref[...]
    for g in range(queries.shape[1] // 128):
        cut = slice(128 * g, 128 * g + 128)
        q_ref[:, cut] = rotate(queries[:, cut], cos, sin).astype(BF)


def head_mask(shape, head):
    return lax.broadcasted_iota(jnp.int32, shape, 1) // HEAD_DIM == head


def fold_scale(q, head):
    return jnp.where(head_mask(q.shape, head), q, jnp.zeros_like(q)) * jnp.asarray(HEAD_DIM**-0.5, BF)


def attend_kernel(q_ref, kn_ref, kf_ref, vn_ref, vf_ref, o_ref, lse_ref):
    q, k, v = q_ref[...], both_halves(kn_ref, kf_ref), both_halves(vn_ref, vf_ref)
    for h in range(2):
        scores = dot(k, fold_scale(q, h), NT)
        top = jnp.max(scores, axis=0, keepdims=True)
        weights = jnp.exp(scores - top)
        total = jnp.sum(weights, axis=0, keepdims=True)
        out = dot(v, weights.astype(BF), TN)
        cut = slice(HEAD_DIM * h, HEAD_DIM * h + HEAD_DIM)
        o_ref[cut, :] = out[cut, :] / total
        lse_ref[0, h : h + 1, :] = top + jnp.log(total)


def middle_kernel(
    svec, x_ref, at_ref, lse_ref, i0, i1, o0, o1, af, as_, acf, acs, b0, b1, b2, b3, dy_ref, gains_ref,
    lo_ref, dm_ref, pay_ref, dat_ref, mine_ref, core_ref, y_ref,
    win, wout, wdown, n2t, attnt, hidt,
):
    width = x_ref.shape[1]
    own = x_ref.shape[0]
    half = width // 8
    ff = wdown.shape[0]
    frows = ff // 4
    every = slice(None)
    for b in range(3):
        cut = slice(b * width, (b + 1) * width)
        spread(svec, ((i0, cut), (i1, cut), (af, as_, every), (acf, acs, every)), half, (0, b * half), win, cut)
    spread(svec, ((o0, every), (o1, every), (af, as_, every), (acf, acs, every)), half, (0, 3 * half), wout, every)
    for j, piece in enumerate((b0, b1, b2, b3)):
        wdown[pl.ds(pl.multiple_of((svec[0] ^ j) * frows, 16), frows), :] = piece[...]

    gain = gains_ref[1:2, :]
    attn_t = at_ref[...]
    attnt[...] = attn_t.astype(BF)
    attn_low = jnp.transpose(attn_t).astype(BF)
    mid = x_ref[...].astype(F32) + dot(attn_low, wout[...])
    xhat, scale = normalise(mid)
    normed = xhat * gain
    n2t[...] = jnp.transpose(normed).astype(BF)
    up = dot(normed.astype(BF), win[...])
    gate, lin = up[:, :ff], up[:, ff:]
    cdf = 0.5 * (1.0 + lax.erf(gate * (2.0**-0.5)))
    act = gate * cdf
    hidden = act * lin
    hidt[...] = jnp.transpose(hidden).astype(BF)
    lo_ref[...] = (mid + dot(hidden.astype(BF), wdown[...])).astype(BF)
    dy = dy_ref[...]
    d_hidden = dot(dy, wdown[...], NT)
    pdf = jnp.exp(-0.5 * gate * gate) * (1.0 / math.sqrt(2.0 * math.pi))
    d_gate = (d_hidden * lin * (cdf + gate * pdf)).astype(BF)
    d_lin = (d_hidden * act).astype(BF)
    d_up = jnp.concatenate([d_gate, d_lin], axis=1)
    d_mid = dy.astype(F32) + norm_back(dot(d_up, win[...], NT), xhat, scale, gain)
    dm_ref[...] = d_mid
    d_branch = d_mid.astype(BF)
    rows = width // 4
    part = 2 * rows + frows
    for j, (to_ref, begin) in enumerate(((mine_ref, 0), (core_ref, 0), (y_ref, 0), (y_ref, part))):
        q = svec[0] ^ j
        at = pl.multiple_of(q * rows, 16)
        to_ref[begin : begin + rows, :] = n2t[pl.ds(at, rows), :]
        to_ref[begin + rows : begin + 2 * rows, :] = attnt[pl.ds(at, rows), :]
        to_ref[begin + 2 * rows : begin + part, :] = hidt[pl.ds(pl.multiple_of(q * frows, 16), frows), :]
    d_all = jnp.concatenate([d_up, d_branch, dy], axis=1)
    for b in range(5 * width // 128):
        piece = d_all[:, 128 * b : 128 * b + 128]
        for to_ref, begin in ((core_ref, part), (y_ref, 2 * part)):
            to_ref[begin + b * own : begin + (b + 1) * own, :] = piece
    pay_ref[0, :own, :] = dot(d_branch, wout[...], NT).astype(BF)
    d_attn_t = dot(wout[...], d_branch, NT).astype(BF)
    dat_ref[...] = d_attn_t
    prod = d_attn_t.astype(F32) * attn_t
    for g in range(width // 128):
        stats = []
        for h in range(2):
            begin = 128 * g + HEAD_DIM * h
            delta = jnp.sum(prod[begin : begin + HEAD_DIM, :], axis=0, keepdims=True)
            for row in (lse_ref[g, h : h + 1, :], delta):
                high = row.astype(BF).astype(F32)
                stats += [high, row - high]
        stats = jnp.concatenate(stats + [jnp.zeros((8, own), F32)], axis=0)
        pay_ref[0, own:, 128 * g : 128 * g + 128] = stats.astype(BF)


def middle_grad_kernel(
    svec, mine_ref, core_ref, c_ref, y_ref, cy_ref,
    low_ref, high_ref, left, right, g_in, g_out, g_down,
):
    part = mine_ref.shape[0]
    own = mine_ref.shape[1]
    width = right.shape[1] // 5
    rows = width // 4
    frows = part - 2 * rows
    step, fstep = rows // CHUNKS, frows // CHUNKS
    sources = ((mine_ref, 0, core_ref, part), (c_ref, 0, c_ref, part), (y_ref, 0, y_ref, 2 * part), (cy_ref, part, cy_ref, 2 * part))
    for i, (x_ref, x_at, d_ref, d_at) in enumerate(sources):
        left[:, i * own : (i + 1) * own] = x_ref[x_at : x_at + part, :]
        for b in range(5 * width // 128):
            right[i * own : (i + 1) * own, 128 * b : 128 * b + 128] = d_ref[d_at + b * own : d_at + (b + 1) * own, :]
    g_in[...] = dot(left[:rows, :], right[:, : 3 * width])
    g_out[...] = dot(left[rows : 2 * rows, :], right[:, 3 * width : 4 * width])
    g_down[...] = dot(left[2 * rows :, :], right[:, 4 * width :])
    for spot in reversed(range(CHUNKS)):
        c = spot ^ svec[2]
        at = pl.multiple_of(c * step, 8)
        fat = pl.multiple_of(2 * fstep * (c >> 1) + (fstep - 4) * (c & 1), 8)
        parts = [g_in[pl.ds(at, step), :], g_out[pl.ds(at, step), :], g_down[pl.ds(fat, fstep + 4), :]]
        target = high_ref if spot >= CHUNKS // 2 else low_ref
        target[spot % (CHUNKS // 2)] = fold(parts).astype(BF)


def attend_back_kernel(q_ref, kn_ref, kf_ref, vn_ref, vf_ref, da_ref, dat_ref, at_ref, lse_ref, cos_ref, sin_ref, dq_ref, dkv_ref):
    q, k, v = q_ref[...], both_halves(kn_ref, kf_ref), both_halves(vn_ref, vf_ref)
    own = q.shape[0]
    da = da_ref[0, :own, :]
    prod = dat_ref[...].astype(F32) * at_ref[...]
    d_key, d_value, d_query = 0.0, 0.0, []
    for h in range(2):
        cut = slice(HEAD_DIM * h, HEAD_DIM * h + HEAD_DIM)
        q_scaled = fold_scale(q, h)
        da_head = jnp.where(head_mask(da.shape, h), da, jnp.zeros_like(da))
        probs = jnp.exp(dot(k, q_scaled, NT) - lse_ref[0, h : h + 1, :])
        delta = jnp.sum(prod[cut, :], axis=0, keepdims=True)
        d_scores = (probs * (dot(v, da_head, NT) - delta)).astype(BF)
        d_value += dot(probs.astype(BF), da_head)
        d_key += dot(d_scores, q_scaled)
        d_query.append(dot(d_scores, k, TN))
    dkv_ref[0] = rotate_back(d_key, cos_ref[...], sin_ref[...]).astype(BF)
    dkv_ref[1] = d_value.astype(BF)
    d_q = jnp.where(head_mask(q.shape, 0), d_query[0], d_query[1]) * (HEAD_DIM**-0.5)
    dq_ref[...] = rotate_back(d_q, cos_ref[:own, :], sin_ref[:own, :]).astype(BF)


def attend_keys_kernel(q_ref, k_ref, v_ref, near_ref, far_ref, cos_ref, sin_ref, dk_ref, dv_ref):
    k, v, q = k_ref[...], v_ref[...], q_ref[...]
    own = k.shape[0]
    both = [(r, i) for r in (near_ref, far_ref) for i in range(near_ref.shape[0])]
    da = jnp.concatenate([r[i, :own, :] for r, i in both], axis=0)
    stats = jnp.concatenate([r[i, own:, :].astype(F32) for r, i in both], axis=1)
    d_key, d_value = [], []
    for h in range(2):
        lse = stats[4 * h : 4 * h + 1] + stats[4 * h + 1 : 4 * h + 2]
        delta = stats[4 * h + 2 : 4 * h + 3] + stats[4 * h + 3 : 4 * h + 4]
        v_head = jnp.where(head_mask(v.shape, h), v, jnp.zeros_like(v))
        probs = jnp.exp(dot(fold_scale(k, h), q, NT) - lse)
        d_scores = (probs * (dot(v_head, da, NT) - delta)).astype(BF)
        d_value.append(dot(probs.astype(BF), da))
        d_key.append(dot(d_scores, q))
    first = head_mask(k.shape, 0)
    d_k = jnp.where(first, d_key[0], d_key[1]) * (HEAD_DIM**-0.5)
    dk_ref[...] = rotate_back(d_k, cos_ref[...], sin_ref[...]).astype(BF)
    dv_ref[...] = jnp.where(first, d_value[0], d_value[1]).astype(BF)


def qkv_grad_kernel(svec, near_ref, far_ref, dkv_ref, dq_ref, keep_low, keep_high, send_low, send_high, acc):
    width = near_ref.shape[1]
    rows = width // 4
    step = rows // CHUNKS
    own = dq_ref.shape[0]
    at = pl.program_id(0)
    normed = jnp.where(at >= pl.num_programs(0) // 2, far_ref[...], near_ref[...])
    first = at == 0

    @pl.when(first)
    def _():
        acc[:, :width] = dot(normed[:own], dq_ref[...], TN)
        for b in range(2):
            acc[:, (b + 1) * width : (b + 2) * width] = dot(normed, dkv_ref[b], TN)

    @pl.when(jnp.logical_not(first))
    def _():
        for b in range(2):
            acc[:, (b + 1) * width : (b + 2) * width] += dot(normed, dkv_ref[b], TN)

    @pl.when(pl.program_id(0) == pl.num_programs(0) - 1)
    def _():
        for keep, low_ref, high_ref in ((1, send_low, send_high), (0, keep_low, keep_high)):
            for spot in range(2 * CHUNKS):
                u, c = chunk_at(svec, keep, spot)
                at = pl.multiple_of((svec[0] ^ (2 * u + keep)) * rows + c * step, 8)
                target = high_ref if spot >= CHUNKS else low_ref
                target[spot % CHUNKS] = fold([acc[pl.ds(at, step), :]]).astype(BF)


def tokens_grad_kernel(x_ref, dq_ref, dk_ref, dv_ref, w_ref, gains_ref, dm_ref, out_ref):
    d_proj = jnp.concatenate([dq_ref[...], dk_ref[...], dv_ref[...]], axis=1)
    d_normed = dot(d_proj, w_ref[...], NT)
    xhat, scale = normalise(x_ref[...].astype(F32))
    out_ref[...] = dm_ref[...] + norm_back(d_normed, xhat, scale, gains_ref[0:1, :])


def chunk_of(mark, keep_ref, recv_ref, chunk):
    there = (chunk ^ mark) >= CHUNKS // 2
    return jnp.where(there, recv_ref[0].astype(F32), keep_ref[0].astype(F32))


def gain_rows(product, gain, gain_ref):
    at, rows, cols = pl.program_id(0), product.shape[0], gain_ref.shape[1]
    total = jnp.sum(product, axis=1, keepdims=True)
    row = lax.broadcasted_iota(jnp.int32, (rows, cols), 0)
    col = lax.broadcasted_iota(jnp.int32, (rows, cols), 1)
    part = jnp.sum(jnp.where(col == row + at * rows, total, 0.0), axis=0, keepdims=True) / gain

    @pl.when(at == 0)
    def _():
        gain_ref[...] = part

    @pl.when(at > 0)
    def _():
        gain_ref[...] += part


def finish_first_kernel(svec, ka, ra, kb, rb, w_ref, own_gain, in_ref, out_ref, down_ref, gain_ref, *, step, fstep, width):
    shapes = ((step, 3 * width), (step, width), (fstep + 4, width))
    at = 2 * pl.program_id(0)
    parts_a = unfold(chunk_of(svec[2], ka, ra, at), shapes)
    parts_b = unfold(chunk_of(svec[2], kb, rb, at + 1), shapes)
    both = [jnp.concatenate([a, b], axis=0) for a, b in zip(parts_a[:2], parts_b[:2])]
    in_ref[...] = both[0]
    out_ref[...] = both[1]
    down_ref[...] = jnp.concatenate([parts_a[2], parts_b[2][8:]], axis=0)
    gain_rows(w_ref[...].astype(F32) * both[0], own_gain[1:2, :], gain_ref)


def finish_second_kernel(svec, ka, ra, kb, rb, w_ref, own_gain, out_ref, gain_ref, *, step, width):
    shapes = ((step, 3 * width),)
    at = 2 * pl.program_id(0)
    chunks = [chunk_of(svec[3], ka, ra, at), chunk_of(svec[3], kb, rb, at + 1)]
    grad = jnp.concatenate([unfold(c, shapes)[0] for c in chunks], axis=0)
    out_ref[...] = grad
    gain_rows(w_ref[...].astype(F32) * grad, own_gain[0:1, :], gain_ref)


class Links:
    def __init__(self, n_dp, n_ctx):
        self.n_dp, self.n_ctx = n_dp, n_ctx
        self.bits = n_ctx.bit_length() - 1
        rise = list(range(self.bits))
        self.orders = (rise, rise[1:] + rise[:1])

    def swap(self, value, dims):
        pairs = []
        for d in range(self.n_dp):
            dim = dims[d & 1]
            for c in range(self.n_ctx):
                if dim == "core":
                    to = (d ^ 1, c)
                elif dim == "y":
                    to = (d ^ 2, c)
                else:
                    to = (d, c ^ (1 << dim))
                pairs.append((d * self.n_ctx + c, to[0] * self.n_ctx + to[1]))
        return lax.ppermute(value, ("dp", "ctx"), pairs)

    def both(self, step):
        return (self.orders[0][step], self.orders[1][step])


def add_low(left, right):
    return (left.astype(F32) + right.astype(F32)).astype(BF)


def after(value, *others):
    return lax.optimization_barrier((value,) + others)[0]


class Chain:
    def __init__(self, links, walks, keep, send):
        self.links = links
        self.halvings = list(zip(*walks))
        self.whole = [(b, b) for b in range(CHUNK_BITS, links.bits)]
        self.doublings = list(zip(*[[d for d in reversed(w) if d != "y"] for w in walks]))
        self.keep = keep
        if isinstance(keep, tuple):
            high = links.swap(send[1], ("core", "core"))
            self.recv = (links.swap(send[0], ("core", "core")), high)
            self.at = 0
        else:
            self.recv = links.swap(send, self.halvings[0])
            self.at = 1

    def step(self, *others):
        keep, recv, links, at = self.keep, self.recv, self.links, self.at
        if others:
            keep = after(keep, *others) if at else (keep[0], after(keep[1], *others))
        self.at += 1
        if at == 0:
            send = add_low(keep[1], recv[1])
            self.keep = add_low(keep[0], recv[0])
            self.recv = links.swap(send, self.halvings[0])
            return send
        if at < len(self.halvings):
            half = keep.shape[0] // 2
            send = add_low(keep[half:], recv[half:])
            self.keep = add_low(after(keep, send)[:half], recv[:half])
            self.recv = links.swap(send, self.halvings[at])
            return send
        at -= len(self.halvings)
        if at <= len(self.whole):
            self.keep = add_low(keep, recv)
        else:
            self.keep = jnp.concatenate([keep, recv], axis=0)
        self.recv = links.swap(self.keep, (self.whole + self.doublings)[at])
        return self.keep

    def more(self):
        return self.at < len(self.halvings + self.whole + self.doublings)


def on_device(tokens, w_qkv, w_attn_out, w_in, w_down, gain_attn, gain_mlp, cotangent, *, n_dp, n_ctx):
    links = Links(n_dp, n_ctx)
    own, width = tokens.shape
    rows = w_qkv.shape[0]
    frows = w_down.shape[0]
    ff = frows * n_dp
    seq = own * n_ctx
    groups = width // 128
    step, fstep = rows // CHUNKS, frows // CHUNKS
    dp_at = lax.axis_index("dp")
    ctx_at = lax.axis_index("ctx")
    core = dp_at & 1
    upper = dp_at >> 1

    marks = []
    for walks in (FIRST_WALKS, SECOND_WALKS):
        both = []
        for walk in walks:
            bits = [b for b in walk if b != "y"]
            both.append(sum(((ctx_at >> b) & 1) << (CHUNK_BITS - 1 - i) for i, b in enumerate(bits)))
        marks += [jnp.where(core == 0, both[0], both[1]), jnp.where(core == 0, both[1], both[0])]
    z_at = (ctx_at >> 1) & 1
    svec = jnp.stack([dp_at, z_at, marks[0], marks[2], marks[3]]).astype(jnp.int32)

    half_rows = rows // 2
    near_sides = ("core", "core")

    def z_half(cols):
        return pl.BlockSpec((half_rows, cols), lambda i, s: (s[1], 0))

    qkv_y = links.swap(w_qkv, ("y", "y"))
    pair = jnp.concatenate([tokens, links.swap(tokens, links.both(links.bits - 1))], axis=0)
    qkv_c = links.swap(w_qkv, near_sides)
    gains = jnp.stack([gain_attn, gain_mlp]).astype(F32)
    gains_c = links.swap(gains, near_sides)
    gains_y = links.swap(gains, ("y", "y"))
    gains_cy = links.swap(gains_y, near_sides)

    flips = []
    for order in links.orders:
        at = np.arange(n_ctx)
        flips.append(sum(((at >> i) & 1) << order[links.bits - 1 - i] for i in range(links.bits)).astype(np.int32))
    owner = ctx_at ^ jnp.where(core == 0, jnp.asarray(flips[0]), jnp.asarray(flips[1]))
    owner = after(owner, pair)
    positions = (owner[:, None] * own + jnp.arange(own, dtype=jnp.int32)[None, :]).reshape(seq).astype(F32)
    half = HEAD_DIM // 2
    frequencies = jnp.exp(jnp.arange(half, dtype=F32) * (-2.0 * math.log(THETA) / HEAD_DIM))
    angles = positions[:, None] * frequencies[None, :]
    cos, sin = jnp.cos(angles), jnp.sin(angles)
    cos = jnp.concatenate([cos] * 4, axis=1)
    sin = jnp.concatenate([-sin, sin, -sin, sin], axis=1)

    half_up = pl.pallas_call(
        pack_up_kernel,
        grid_spec=pltpu.PrefetchScalarGridSpec(
            num_scalar_prefetch=1,
            grid=(1,),
            in_specs=[z_half(3 * width), z_half(width)],
            out_specs=whole((4 * half_rows, width)),
        ),
        out_shape=jax.ShapeDtypeStruct((4 * half_rows, width), BF),
        compiler_params=params(),
        cost_estimate=cost(COSTS["pack_up"]),
        name="pack_up",
    )(svec, after(w_in, cos, sin), w_attn_out)
    everyone = pair
    for i in reversed(range(1, links.bits - 1)):
        come = after(links.swap(everyone, links.both(i)), half_up, gains_y)
        everyone = jnp.concatenate([everyone, come], axis=0)
    far = links.swap(everyone, links.both(0))
    qkv_y = after(qkv_y, everyone)
    qkv_cy = links.swap(qkv_y, near_sides)
    up_first = links.swap(after(half_up, qkv_y), ("y", "y"))

    block = math.gcd(seq // 2, 256)
    turn = seq // 2 // block
    table = pl.BlockSpec((block, 128), lambda i, *_: (i, 0))
    rows_of = pl.BlockSpec((block, width), lambda i, *_: (i, 0))
    half_seq = jax.ShapeDtypeStruct((seq // 2, width), BF)
    normed_near, queries, keys_near, values_near, full_qkv, gains_full = pl.pallas_call(
        functools.partial(qkv_near_kernel, own=own),
        grid_spec=pltpu.PrefetchScalarGridSpec(
            num_scalar_prefetch=1,
            grid=(turn,),
            in_specs=[rows_of] + [whole(w_qkv.shape)] * 4 + [whole((2, rows))] * 4 + [table] * 2,
            out_specs=[rows_of, whole((own, width)), rows_of, rows_of, whole((width, 3 * width)), whole((2, width))],
        ),
        out_shape=[
            half_seq,
            jax.ShapeDtypeStruct((own, width), BF),
            half_seq,
            half_seq,
            jax.ShapeDtypeStruct((width, 3 * width), BF),
            jax.ShapeDtypeStruct((2, width), F32),
        ],
        compiler_params=params(),
        cost_estimate=cost(COSTS["qkv_near"]),
        name="qkv_near",
    )(svec, everyone, w_qkv, qkv_c, qkv_y, qkv_cy, gains, gains_c, gains_y, gains_cy, cos, sin)
    in_c, out_c, down_c = (links.swap(after(w, everyone), near_sides) for w in (w_in, w_attn_out, w_down))

    far_table = pl.BlockSpec((block, 128), lambda i, *_: (i + turn, 0))
    up_first = after(up_first, full_qkv)
    up_second = links.swap(up_first, (1, 1))
    down_y = links.swap(after(w_down, up_first), ("y", "y"))
    up_cf = links.swap(up_first, near_sides)
    normed_far, keys_far, values_far = pl.pallas_call(
        qkv_far_kernel,
        grid=(turn,),
        in_specs=[rows_of, pl.BlockSpec((width, 3 * width), lambda i: (0, 0)), whole((2, width)), far_table, far_table],
        out_specs=[rows_of] * 3,
        out_shape=[half_seq] * 3,
        compiler_params=params(),
        cost_estimate=cost(COSTS["qkv_far"]),
        name="qkv_far",
    )(after(far, up_first, in_c, out_c, down_c), full_qkv, gains_full, cos, sin)
    keys = (keys_near, keys_far)
    values = (values_near, values_far)

    own_pair = pl.BlockSpec((own, 128), lambda g: (0, g))
    seq_pair = pl.BlockSpec((seq, 128), lambda g: (0, g))
    half_pair = pl.BlockSpec((seq // 2, 128), lambda g: (0, g))
    turned_pair = pl.BlockSpec((128, own), lambda g: (g, 0))
    lse_pair = pl.BlockSpec((1, 8, own), lambda g: (g, 0, 0))
    attn_t, lse = pl.pallas_call(
        attend_kernel,
        grid=(groups,),
        in_specs=[own_pair] + [half_pair] * 4,
        out_specs=[turned_pair, lse_pair],
        out_shape=[jax.ShapeDtypeStruct((width, own), F32), jax.ShapeDtypeStruct((groups, 8, own), F32)],
        compiler_params=params(),
        cost_estimate=cost(COSTS["attend"]),
        name="attend",
    )(queries, *keys, *values)
    up_second = after(up_second, attn_t)
    down_y = after(down_y, attn_t)

    up_cs = links.swap(up_second, near_sides)
    down_cy = links.swap(down_y, near_sides)


    vm = pl.BlockSpec(memory_space=pltpu.VMEM)
    length = (3 * step * 4 * width // 3 + (fstep + 4) * width) // 16
    part = 2 * rows + frows
    layer_out, d_mid, payload, d_attn_t, share_mine, share_core, share_y = pl.pallas_call(
        middle_kernel,
        in_specs=[pl.BlockSpec(memory_space=pltpu.SMEM)] + [vm] * 17,
        out_specs=[vm] * 7,
        out_shape=[
            jax.ShapeDtypeStruct((own, width), BF),
            jax.ShapeDtypeStruct((own, width), F32),
            jax.ShapeDtypeStruct((1, own + 16, width), BF),
            jax.ShapeDtypeStruct((width, own), BF),
            jax.ShapeDtypeStruct((part, own), BF),
            jax.ShapeDtypeStruct((part + 5 * width, own), BF),
            jax.ShapeDtypeStruct((2 * part + 5 * width, own), BF),
        ],
        scratch_shapes=[
            pltpu.VMEM((width, 3 * width), BF),
            pltpu.VMEM((width, width), BF),
            pltpu.VMEM((ff, width), BF),
            pltpu.VMEM((width, own), BF),
            pltpu.VMEM((width, own), BF),
            pltpu.VMEM((ff, own), BF),
        ],
        compiler_params=params(),
        cost_estimate=cost(COSTS["middle"]),
        name="middle",
    )(
        svec, tokens, attn_t, lse, w_in, in_c, w_attn_out, out_c, up_first, up_second, up_cf, up_cs,
        w_down, down_c, down_y, down_cy, cotangent, gains_full,
    )

    come_y = links.swap(share_y, ("y", "y"))
    come_c = links.swap(share_core, near_sides)

    d_query, d_kv = pl.pallas_call(
        attend_back_kernel,
        grid=(groups,),
        in_specs=[
            own_pair, half_pair, half_pair, half_pair, half_pair,
            pl.BlockSpec((1, own + 16, 128), lambda g: (0, 0, g)), turned_pair, turned_pair, lse_pair,
            whole((seq, 128)), whole((seq, 128)),
        ],
        out_specs=[own_pair, pl.BlockSpec((2, seq, 128), lambda g: (0, 0, g))],
        out_shape=[jax.ShapeDtypeStruct((own, width), BF), jax.ShapeDtypeStruct((2, seq, width), BF)],
        compiler_params=params(),
        cost_estimate=cost(COSTS["attend_back"]),
        name="attend_back",
    )(queries, *keys, *values, payload, d_attn_t, attn_t, lse, cos, sin)

    deep = math.gcd(seq // 2, 1024)
    turns = seq // 2 // deep
    second_parts = pl.pallas_call(
        qkv_grad_kernel,
        grid_spec=pltpu.PrefetchScalarGridSpec(
            num_scalar_prefetch=1,
            grid=(2 * turns,),
            in_specs=[
                pl.BlockSpec((deep, width), lambda i, s: (jnp.minimum(i, turns - 1), 0)),
                pl.BlockSpec((deep, width), lambda i, s: (jnp.maximum(i - turns, 0), 0)),
                pl.BlockSpec((2, deep, width), lambda i, s: (0, i, 0)),
                whole((own, width)),
            ],
            out_specs=[whole((CHUNKS, 16, step * 3 * width // 16))] * 4,
            scratch_shapes=[pltpu.VMEM((width, 3 * width), F32)],
        ),
        out_shape=[jax.ShapeDtypeStruct((CHUNKS, 16, step * 3 * width // 16), BF)] * 4,
        compiler_params=params(),
        cost_estimate=cost(COSTS["qkv_grad"]),
        name="qkv_grad",
    )(svec, normed_near, normed_far, d_kv, d_query)

    second = Chain(links, SECOND_WALKS, second_parts[:2], second_parts[2:])
    every_query = pl.pallas_call(
        queries_kernel,
        grid=(2 * turn,),
        in_specs=[
            pl.BlockSpec((block, width), lambda i: (jnp.minimum(i, turn - 1), 0)),
            pl.BlockSpec((block, width), lambda i: (jnp.maximum(i - turn, 0), 0)),
            pl.BlockSpec((width, width), lambda i: (0, 0)),
            table,
            table,
        ],
        out_specs=rows_of,
        out_shape=jax.ShapeDtypeStruct((seq, width), BF),
        compiler_params=params(),
        cost_estimate=cost(COSTS["every_query"]),
        name="every_query",
    )(after(normed_near, second_parts[0]), normed_far, full_qkv, cos, sin)
    come_y = after(come_y, every_query)
    come_cy = links.swap(come_y, near_sides)
    sent = second.step(come_y)
    first_low, first_high = pl.pallas_call(
        middle_grad_kernel,
        in_specs=[pl.BlockSpec(memory_space=pltpu.SMEM)] + [vm] * 5,
        out_specs=[vm] * 2,
        out_shape=[jax.ShapeDtypeStruct((CHUNKS // 2, 16, length), BF)] * 2,
        scratch_shapes=[
            pltpu.VMEM((part, n_dp * own), BF),
            pltpu.VMEM((n_dp * own, 5 * width), BF),
            pltpu.VMEM((rows, 3 * width), F32),
            pltpu.VMEM((rows, width), F32),
            pltpu.VMEM((frows, width), F32),
        ],
        compiler_params=params(),
        cost_estimate=cost(COSTS["middle_grad"]),
        name="middle_grad",
    )(svec, after(share_mine, sent), share_core, come_c, come_y, come_cy)
    first = Chain(links, FIRST_WALKS, first_low, first_high)
    gathered = links.swap(payload, links.both(links.bits - 1))
    gathered = jnp.concatenate([payload, after(gathered, first_high)], axis=0)
    late = first.step(second.step(gathered))
    late = first.step(second.step(late))
    for i in reversed(range(1, links.bits - 1)):
        come = links.swap(gathered, links.both(i))
        gathered = jnp.concatenate([gathered, after(come, late)], axis=0)
    gathered_far = links.swap(gathered, links.both(0))
    late = gathered
    while first.more() or second.more():
        for chain in (second, first):
            if chain.more():
                late = chain.step(late)

    d_key, d_value = pl.pallas_call(
        attend_keys_kernel,
        grid=(groups,),
        in_specs=[
            seq_pair, own_pair, own_pair,
            pl.BlockSpec((n_ctx // 2, own + 16, 128), lambda g: (0, 0, g)),
            pl.BlockSpec((n_ctx // 2, own + 16, 128), lambda g: (0, 0, g)),
            whole((own, 128)), whole((own, 128)),
        ],
        out_specs=[own_pair, own_pair],
        out_shape=[jax.ShapeDtypeStruct((own, width), BF)] * 2,
        compiler_params=params(),
        cost_estimate=cost(COSTS["attend_keys"]),
        name="attend_keys",
    )(every_query, keys_near, values_near, gathered, after(gathered_far, late), cos, sin)

    tokens_grad = pl.pallas_call(
        tokens_grad_kernel,
        in_specs=[vm] * 7,
        out_specs=vm,
        out_shape=jax.ShapeDtypeStruct((own, width), F32),
        compiler_params=params(),
        cost_estimate=cost(COSTS["tokens_grad"]),
        name="tokens_grad",
    )(tokens, d_query, d_key, d_value, full_qkv, gains_full, d_mid)
    def pair_specs(length, mark):
        half = CHUNKS // 2
        return [
            pl.BlockSpec((1, 16, length), lambda i, s, c=c: (((2 * i + c) ^ s[mark]) % half, 0, 0)) for c in (0, 0, 1, 1)
        ]

    def row_spec(count, cols):
        return pl.BlockSpec((count, cols), lambda i, s: (i, 0))

    qkv_grad, gain_attn_sum = pl.pallas_call(
        functools.partial(finish_second_kernel, step=step, width=width),
        grid_spec=pltpu.PrefetchScalarGridSpec(
            num_scalar_prefetch=1,
            grid=(CHUNKS // 2,),
            in_specs=pair_specs(step * 3 * width // 16, 3) + [row_spec(2 * step, 3 * width), whole((2, rows))],
            out_specs=[row_spec(2 * step, 3 * width), whole((1, rows))],
        ),
        out_shape=[jax.ShapeDtypeStruct((rows, 3 * width), F32), jax.ShapeDtypeStruct((1, rows), F32)],
        compiler_params=params(),
        cost_estimate=cost(COSTS["finish_second"]),
        name="finish_second",
    )(svec, second.keep, after(second.recv, tokens_grad), second.keep, second.recv, w_qkv, gains)

    in_grad, out_grad, down_grad, gain_mlp_sum = pl.pallas_call(
        functools.partial(finish_first_kernel, step=step, fstep=fstep, width=width),
        grid_spec=pltpu.PrefetchScalarGridSpec(
            num_scalar_prefetch=1,
            grid=(CHUNKS // 2,),
            in_specs=pair_specs(length, 2) + [row_spec(2 * step, 3 * width), whole((2, rows))],
            out_specs=[
                row_spec(2 * step, 3 * width),
                row_spec(2 * step, width),
                row_spec(2 * fstep, width),
                whole((1, rows)),
            ],
        ),
        out_shape=[
            jax.ShapeDtypeStruct((rows, 3 * width), F32),
            jax.ShapeDtypeStruct((rows, width), F32),
            jax.ShapeDtypeStruct((frows, width), F32),
            jax.ShapeDtypeStruct((1, rows), F32),
        ],
        compiler_params=params(),
        cost_estimate=cost(COSTS["finish_first"]),
        name="finish_first",
    )(svec, first.keep, after(first.recv, qkv_grad), first.keep, first.recv, w_in, gains)

    return (
        layer_out,
        tokens_grad,
        qkv_grad,
        out_grad,
        in_grad,
        down_grad,
        gain_attn_sum.reshape(rows),
        gain_mlp_sum.reshape(rows),
    )


def solution(mesh):
    return jax.shard_map(
        functools.partial(on_device, n_dp=mesh.shape["dp"], n_ctx=mesh.shape["ctx"]),
        mesh=mesh,
        in_specs=(
            P(("dp", "ctx"), None),
            P("dp", None),
            P("dp", None),
            P("dp", None),
            P("dp", None),
            P("dp"),
            P("dp"),
            P(("dp", "ctx"), None),
        ),
        out_specs=(
            P(("dp", "ctx"), None),
            P(("dp", "ctx"), None),
            P("dp", None),
            P("dp", None),
            P("dp", None),
            P("dp", None),
            P("dp"),
            P("dp"),
        ),
        check_vma=False,
    )
```

```python
import functools
import math

import jax
import jax.numpy as jnp
import numpy as np
from jax import lax
from jax.experimental import pallas as pl
from jax.experimental.pallas import tpu as pltpu
from jax.sharding import PartitionSpec as P

HEADS = 12
HEAD_DIM = 64
THETA = 160000.0
EPS = 1e-05
CHUNK_BITS = 2
CHUNKS = 1 << CHUNK_BITS
BF = jnp.bfloat16
F32 = jnp.float32
COSTS = {
    "pack_up": 0.5,
    "qkv_near": 0.5,
    "qkv_far": 0.5,
    "attend": 0.5,
    "middle": 0.5,
    "middle_grad": 0.5,
    "every_query": 0.5,
    "attend_back": 0.5,
    "qkv_grad": 0.5,
    "attend_keys": 0.5,
    "tokens_grad": 0.5,
    "finish_first": 0.5,
    "finish_second": 0.5,
}
FIRST_WALKS = ((0, 1), (1, 0))
SECOND_WALKS = (("y", 0, 1), (1, "y", 0))
VMEM_LIMIT = 58 * 1024 * 1024


def whole(shape):
    return pl.BlockSpec(shape, lambda *_: (0,) * len(shape))


def params(limit=VMEM_LIMIT):
    return pltpu.CompilerParams(vmem_limit_bytes=limit)


def cost(micros):
    return pl.CostEstimate(flops=int(micros * 1.15e9), bytes_accessed=0, transcendentals=0)


def dot(left, right, dims=((1,), (0,))):
    return lax.dot_general(left, right, (dims, ((), ())), preferred_element_type=F32)


NT = ((1,), (1,))
TN = ((0,), (0,))


def normalise(values):
    center = values - jnp.mean(values, axis=-1, keepdims=True)
    spread = jnp.mean(center * center, axis=-1, keepdims=True)
    scale = lax.rsqrt(spread + EPS)
    return center * scale, scale


def norm_back(grad, xhat, scale, gain):
    inner = grad * gain
    return scale * (
        inner
        - jnp.mean(inner, axis=-1, keepdims=True)
        - xhat * jnp.mean(inner * xhat, axis=-1, keepdims=True)
    )


def swap_halves(values):
    lane = lax.broadcasted_iota(jnp.int32, values.shape, 1)
    return jnp.where(lane % 64 < 32, pltpu.roll(values, 96, 1), pltpu.roll(values, 32, 1))


def rotate(values, cos, sin):
    return values * cos + swap_halves(values) * sin


def rotate_back(values, cos, sin):
    return values * cos - swap_halves(values) * sin


def fold(pieces):
    rows = [p[8 * i : 8 * i + 8] for p in pieces for i in range(p.shape[0] // 8)]
    flat = jnp.concatenate(rows, axis=1)
    half = flat.shape[1] // 2
    return jnp.concatenate([flat[:, :half], flat[:, half:]], axis=0)


def unfold(block, shapes):
    flat = jnp.concatenate([block[:8], block[8:]], axis=1)
    out, at = [], 0
    for rows, cols in shapes:
        parts = []
        for _ in range(rows // 8):
            parts.append(flat[:, at : at + cols])
            at += cols
        out.append(jnp.concatenate(parts, axis=0))
    return out


def chunk_at(svec, keep, spot):
    found = []
    for walk in SECOND_WALKS:
        low = CHUNK_BITS - walk.index("y")
        rel = ((spot >> (low + 1)) << low) | (spot & ((1 << low) - 1))
        found.append(((spot >> low) & 1, rel))
    core = (svec[0] & 1) ^ keep
    upper = jnp.where(core == 0, found[0][0], found[1][0])
    return upper, jnp.where(core == 0, found[0][1], found[1][1]) ^ svec[3 + keep]


def spread(svec, pieces, half, begins, to_ref, to_cols):
    for j, parts in enumerate(pieces):
        halved = len(parts) == 3
        for h in range(2):
            to = (svec[0] ^ j) * (2 * half) + (svec[1] ^ h if halved else h) * half
            at = begins[1] if halved else begins[0] + h * half
            part = parts[h if halved else 0]
            to_ref[pl.ds(pl.multiple_of(to, 16), half), to_cols] = part[at : at + half, parts[-1]]


def pack_up_kernel(svec, in_ref, w_ref, out_ref):
    half, width = w_ref.shape
    for b in range(3):
        out_ref[b * half : (b + 1) * half, :] = in_ref[:, b * width : (b + 1) * width]
    out_ref[3 * half :, :] = w_ref[...]


def project(x_ref, gain, cos_ref, sin_ref, w_ref, n_ref, k_ref, v_ref):
    width = n_ref.shape[1]
    xhat, _ = normalise(x_ref[...].astype(F32))
    normed = (xhat * gain).astype(BF)
    n_ref[...] = normed
    cos, sin = cos_ref[...], sin_ref[...]
    keys = dot(normed, w_ref[:, width : 2 * width])
    for g in range(width // 128):
        cut = slice(128 * g, 128 * g + 128)
        k_ref[:, cut] = rotate(keys[:, cut], cos, sin).astype(BF)
    v_ref[...] = dot(normed, w_ref[:, 2 * width :]).astype(BF)
    return normed, cos, sin


def qkv_near_kernel(
    svec, x_ref, w0, w1, w2, w3, g0_ref, g1_ref, g2_ref, g3_ref, cos_ref, sin_ref,
    n_ref, q_ref, k_ref, v_ref, w_ref, gain_ref, *, own,
):
    rows = w_ref.shape[0] // 4
    width = n_ref.shape[1]
    first = pl.program_id(0) == 0

    @pl.when(first)
    def _():
        for j, piece in enumerate((w0, w1, w2, w3)):
            w_ref[pl.ds(pl.multiple_of((svec[0] ^ j) * rows, 16), rows), :] = piece[...]
        g = [r[:, :rows] for r in (g0_ref, g1_ref, g2_ref, g3_ref)]
        core, upper = svec[0] & 1, svec[0] >> 1
        near = jnp.where(core == 0, jnp.concatenate([g[0], g[1]], axis=1), jnp.concatenate([g[1], g[0]], axis=1))
        far = jnp.where(core == 0, jnp.concatenate([g[2], g[3]], axis=1), jnp.concatenate([g[3], g[2]], axis=1))
        full = jnp.where(upper == 0, jnp.concatenate([near, far], axis=1), jnp.concatenate([far, near], axis=1))
        gain_ref[...] = full

    normed, cos, sin = project(x_ref, gain_ref[0:1, :], cos_ref, sin_ref, w_ref, n_ref, k_ref, v_ref)

    @pl.when(first)
    def _():
        queries = dot(normed[:own], w_ref[:, :width])
        for g in range(width // 128):
            cut = slice(128 * g, 128 * g + 128)
            q_ref[:, cut] = rotate(queries[:, cut], cos[:own], sin[:own]).astype(BF)


def qkv_far_kernel(x_ref, w_ref, gain_ref, cos_ref, sin_ref, n_ref, k_ref, v_ref):
    project(x_ref, gain_ref[0:1, :], cos_ref, sin_ref, w_ref, n_ref, k_ref, v_ref)


def both_halves(near_ref, far_ref):
    return jnp.concatenate([near_ref[...], far_ref[...]], axis=0)


def queries_kernel(near_ref, far_ref, w_ref, cos_ref, sin_ref, q_ref):
    there = pl.program_id(0) >= pl.num_programs(0) // 2
    queries = dot(jnp.where(there, far_ref[...], near_ref[...]), w_ref[...])
    cos, sin = cos_ref[...], sin_ref[...]
    for g in range(queries.shape[1] // 128):
        cut = slice(128 * g, 128 * g + 128)
        q_ref[:, cut] = rotate(queries[:, cut], cos, sin).astype(BF)


def head_mask(shape, head):
    return lax.broadcasted_iota(jnp.int32, shape, 1) // HEAD_DIM == head


def fold_scale(q, head):
    return jnp.where(head_mask(q.shape, head), q, jnp.zeros_like(q)) * jnp.asarray(HEAD_DIM**-0.5, BF)


def attend_kernel(q_ref, kn_ref, kf_ref, vn_ref, vf_ref, o_ref, lse_ref):
    q, k, v = q_ref[...], both_halves(kn_ref, kf_ref), both_halves(vn_ref, vf_ref)
    for h in range(2):
        scores = dot(k, fold_scale(q, h), NT)
        top = jnp.max(scores, axis=0, keepdims=True)
        weights = jnp.exp(scores - top)
        total = jnp.sum(weights, axis=0, keepdims=True)
        out = dot(v, weights.astype(BF), TN)
        cut = slice(HEAD_DIM * h, HEAD_DIM * h + HEAD_DIM)
        o_ref[cut, :] = out[cut, :] / total
        lse_ref[0, h : h + 1, :] = top + jnp.log(total)


def middle_kernel(
    svec, x_ref, at_ref, lse_ref, i0, i1, o0, o1, af, as_, acf, acs, b0, b1, b2, b3, dy_ref, gains_ref,
    lo_ref, dm_ref, pay_ref, dat_ref, mine_ref, core_ref, y_ref,
    win, wout, wdown, n2t, attnt, hidt,
):
    width = x_ref.shape[1]
    own = x_ref.shape[0]
    half = width // 8
    ff = wdown.shape[0]
    frows = ff // 4
    every = slice(None)
    for b in range(3):
        cut = slice(b * width, (b + 1) * width)
        spread(svec, ((i0, cut), (i1, cut), (af, as_, every), (acf, acs, every)), half, (0, b * half), win, cut)
    spread(svec, ((o0, every), (o1, every), (af, as_, every), (acf, acs, every)), half, (0, 3 * half), wout, every)
    for j, piece in enumerate((b0, b1, b2, b3)):
        wdown[pl.ds(pl.multiple_of((svec[0] ^ j) * frows, 16), frows), :] = piece[...]

    gain = gains_ref[1:2, :]
    attn_t = at_ref[...]
    attnt[...] = attn_t.astype(BF)
    attn_low = jnp.transpose(attn_t).astype(BF)
    mid = x_ref[...].astype(F32) + dot(attn_low, wout[...])
    xhat, scale = normalise(mid)
    normed = xhat * gain
    n2t[...] = jnp.transpose(normed).astype(BF)
    up = dot(normed.astype(BF), win[...])
    gate, lin = up[:, :ff], up[:, ff:]
    cdf = 0.5 * (1.0 + lax.erf(gate * (2.0**-0.5)))
    act = gate * cdf
    hidden = act * lin
    hidt[...] = jnp.transpose(hidden).astype(BF)
    lo_ref[...] = (mid + dot(hidden.astype(BF), wdown[...])).astype(BF)
    dy = dy_ref[...]
    d_hidden = dot(dy, wdown[...], NT)
    pdf = jnp.exp(-0.5 * gate * gate) * (1.0 / math.sqrt(2.0 * math.pi))
    d_gate = (d_hidden * lin * (cdf + gate * pdf)).astype(BF)
    d_lin = (d_hidden * act).astype(BF)
    d_up = jnp.concatenate([d_gate, d_lin], axis=1)
    d_mid = dy.astype(F32) + norm_back(dot(d_up, win[...], NT), xhat, scale, gain)
    dm_ref[...] = d_mid
    d_branch = d_mid.astype(BF)
    rows = width // 4
    part = 2 * rows + frows
    for j, (to_ref, begin) in enumerate(((mine_ref, 0), (core_ref, 0), (y_ref, 0), (y_ref, part))):
        q = svec[0] ^ j
        at = pl.multiple_of(q * rows, 16)
        to_ref[begin : begin + rows, :] = n2t[pl.ds(at, rows), :]
        to_ref[begin + rows : begin + 2 * rows, :] = attnt[pl.ds(at, rows), :]
        to_ref[begin + 2 * rows : begin + part, :] = hidt[pl.ds(pl.multiple_of(q * frows, 16), frows), :]
    d_all = jnp.concatenate([d_up, d_branch, dy], axis=1)
    for b in range(5 * width // 128):
        piece = d_all[:, 128 * b : 128 * b + 128]
        for to_ref, begin in ((core_ref, part), (y_ref, 2 * part)):
            to_ref[begin + b * own : begin + (b + 1) * own, :] = piece
    pay_ref[0, :own, :] = dot(d_branch, wout[...], NT).astype(BF)
    d_attn_t = dot(wout[...], d_branch, NT).astype(BF)
    dat_ref[...] = d_attn_t
    prod = d_attn_t.astype(F32) * attn_t
    for g in range(width // 128):
        stats = []
        for h in range(2):
            begin = 128 * g + HEAD_DIM * h
            delta = jnp.sum(prod[begin : begin + HEAD_DIM, :], axis=0, keepdims=True)
            for row in (lse_ref[g, h : h + 1, :], delta):
                high = row.astype(BF).astype(F32)
                stats += [high, row - high]
        stats = jnp.concatenate(stats + [jnp.zeros((8, own), F32)], axis=0)
        pay_ref[0, own:, 128 * g : 128 * g + 128] = stats.astype(BF)


def middle_grad_kernel(
    svec, mine_ref, core_ref, c_ref, y_ref, cy_ref,
    low_ref, high_ref, left, right, g_in, g_out, g_down,
):
    part = mine_ref.shape[0]
    own = mine_ref.shape[1]
    width = right.shape[1] // 5
    rows = width // 4
    frows = part - 2 * rows
    step, fstep = rows // CHUNKS, frows // CHUNKS
    sources = ((mine_ref, 0, core_ref, part), (c_ref, 0, c_ref, part), (y_ref, 0, y_ref, 2 * part), (cy_ref, part, cy_ref, 2 * part))
    for i, (x_ref, x_at, d_ref, d_at) in enumerate(sources):
        left[:, i * own : (i + 1) * own] = x_ref[x_at : x_at + part, :]
        for b in range(5 * width // 128):
            right[i * own : (i + 1) * own, 128 * b : 128 * b + 128] = d_ref[d_at + b * own : d_at + (b + 1) * own, :]
    g_in[...] = dot(left[:rows, :], right[:, : 3 * width])
    g_out[...] = dot(left[rows : 2 * rows, :], right[:, 3 * width : 4 * width])
    g_down[...] = dot(left[2 * rows :, :], right[:, 4 * width :])
    for spot in reversed(range(CHUNKS)):
        c = spot ^ svec[2]
        at = pl.multiple_of(c * step, 8)
        fat = pl.multiple_of(c * fstep, 8)
        parts = [g_in[pl.ds(at, step), :], g_out[pl.ds(at, step), :], g_down[pl.ds(fat, fstep), :]]
        target = high_ref if spot >= CHUNKS // 2 else low_ref
        target[spot % (CHUNKS // 2)] = fold(parts).astype(BF)


def attend_back_kernel(q_ref, kn_ref, kf_ref, vn_ref, vf_ref, da_ref, dat_ref, at_ref, lse_ref, cos_ref, sin_ref, dq_ref, dkv_ref):
    q, k, v = q_ref[...], both_halves(kn_ref, kf_ref), both_halves(vn_ref, vf_ref)
    own = q.shape[0]
    da = da_ref[0, :own, :]
    prod = dat_ref[...].astype(F32) * at_ref[...]
    d_key, d_value, d_query = 0.0, 0.0, []
    for h in range(2):
        cut = slice(HEAD_DIM * h, HEAD_DIM * h + HEAD_DIM)
        q_scaled = fold_scale(q, h)
        da_head = jnp.where(head_mask(da.shape, h), da, jnp.zeros_like(da))
        probs = jnp.exp(dot(k, q_scaled, NT) - lse_ref[0, h : h + 1, :])
        delta = jnp.sum(prod[cut, :], axis=0, keepdims=True)
        d_scores = (probs * (dot(v, da_head, NT) - delta)).astype(BF)
        d_value += dot(probs.astype(BF), da_head)
        d_key += dot(d_scores, q_scaled)
        d_query.append(dot(d_scores, k, TN))
    dkv_ref[0] = rotate_back(d_key, cos_ref[...], sin_ref[...]).astype(BF)
    dkv_ref[1] = d_value.astype(BF)
    d_q = jnp.where(head_mask(q.shape, 0), d_query[0], d_query[1]) * (HEAD_DIM**-0.5)
    dq_ref[...] = rotate_back(d_q, cos_ref[:own, :], sin_ref[:own, :]).astype(BF)


def attend_keys_kernel(q_ref, k_ref, v_ref, near_ref, far_ref, cos_ref, sin_ref, dk_ref, dv_ref):
    k, v, q = k_ref[...], v_ref[...], q_ref[...]
    own = k.shape[0]
    both = [(r, i) for r in (near_ref, far_ref) for i in range(near_ref.shape[0])]
    da = jnp.concatenate([r[i, :own, :] for r, i in both], axis=0)
    stats = jnp.concatenate([r[i, own:, :].astype(F32) for r, i in both], axis=1)
    d_key, d_value = [], []
    for h in range(2):
        lse = stats[4 * h : 4 * h + 1] + stats[4 * h + 1 : 4 * h + 2]
        delta = stats[4 * h + 2 : 4 * h + 3] + stats[4 * h + 3 : 4 * h + 4]
        v_head = jnp.where(head_mask(v.shape, h), v, jnp.zeros_like(v))
        probs = jnp.exp(dot(fold_scale(k, h), q, NT) - lse)
        d_scores = (probs * (dot(v_head, da, NT) - delta)).astype(BF)
        d_value.append(dot(probs.astype(BF), da))
        d_key.append(dot(d_scores, q))
    first = head_mask(k.shape, 0)
    d_k = jnp.where(first, d_key[0], d_key[1]) * (HEAD_DIM**-0.5)
    dk_ref[...] = rotate_back(d_k, cos_ref[...], sin_ref[...]).astype(BF)
    dv_ref[...] = jnp.where(first, d_value[0], d_value[1]).astype(BF)


def qkv_grad_kernel(svec, near_ref, far_ref, dkv_ref, dq_ref, keep_low, keep_high, send_low, send_high, acc):
    width = near_ref.shape[1]
    rows = width // 4
    step = rows // CHUNKS
    own = dq_ref.shape[0]
    at = pl.program_id(0)
    normed = jnp.where(at >= pl.num_programs(0) // 2, far_ref[...], near_ref[...])
    first = at == 0

    @pl.when(first)
    def _():
        acc[:, :width] = dot(normed[:own], dq_ref[...], TN)
        for b in range(2):
            acc[:, (b + 1) * width : (b + 2) * width] = dot(normed, dkv_ref[b], TN)

    @pl.when(jnp.logical_not(first))
    def _():
        for b in range(2):
            acc[:, (b + 1) * width : (b + 2) * width] += dot(normed, dkv_ref[b], TN)

    @pl.when(pl.program_id(0) == pl.num_programs(0) - 1)
    def _():
        for keep, low_ref, high_ref in ((1, send_low, send_high), (0, keep_low, keep_high)):
            for spot in range(2 * CHUNKS):
                u, c = chunk_at(svec, keep, spot)
                at = pl.multiple_of((svec[0] ^ (2 * u + keep)) * rows + c * step, 8)
                target = high_ref if spot >= CHUNKS else low_ref
                target[spot % CHUNKS] = fold([acc[pl.ds(at, step), :]]).astype(BF)


def tokens_grad_kernel(x_ref, dq_ref, dk_ref, dv_ref, w_ref, gains_ref, dm_ref, out_ref):
    d_proj = jnp.concatenate([dq_ref[...], dk_ref[...], dv_ref[...]], axis=1)
    d_normed = dot(d_proj, w_ref[...], NT)
    xhat, scale = normalise(x_ref[...].astype(F32))
    out_ref[...] = dm_ref[...] + norm_back(d_normed, xhat, scale, gains_ref[0:1, :])


def gain_rows(product, gain, chunk, before, gain_ref):
    rows, cols = product.shape[0], gain_ref.shape[1]
    total = jnp.sum(product, axis=1, keepdims=True)
    row = lax.broadcasted_iota(jnp.int32, (rows, cols), 0)
    col = lax.broadcasted_iota(jnp.int32, (rows, cols), 1)
    part = jnp.sum(jnp.where(col == row + chunk * rows, total, 0.0), axis=0, keepdims=True) / gain
    first = pl.program_id(0) == 0

    @pl.when(first)
    def _():
        gain_ref[...] = part + before

    @pl.when(jnp.logical_not(first))
    def _():
        gain_ref[...] += part


def finish_kernel(svec, part_ref, w_ref, own_gain, *refs, shapes, mark, row, begin):
    grads = unfold(part_ref[0].astype(F32), shapes)
    outs = refs[1 + len(shapes) :] if begin else refs
    for out_ref, grad in zip(outs, grads):
        out_ref[...] = grad
    before = refs[0][...] if begin else 0.0
    chunk = (pl.program_id(0) + begin) ^ svec[mark]
    gain_rows(w_ref[...].astype(F32) * grads[0], own_gain[row : row + 1, :], chunk, before, outs[-1])


class Links:
    def __init__(self, n_dp, n_ctx):
        self.n_dp, self.n_ctx = n_dp, n_ctx
        self.bits = n_ctx.bit_length() - 1
        rise = list(range(self.bits))
        self.orders = (rise, rise[1:] + rise[:1])

    def swap(self, value, dims):
        pairs = []
        for d in range(self.n_dp):
            dim = dims[d & 1]
            for c in range(self.n_ctx):
                if dim == "core":
                    to = (d ^ 1, c)
                elif dim == "y":
                    to = (d ^ 2, c)
                else:
                    to = (d, c ^ (1 << dim))
                pairs.append((d * self.n_ctx + c, to[0] * self.n_ctx + to[1]))
        return lax.ppermute(value, ("dp", "ctx"), pairs)

    def both(self, step):
        return (self.orders[0][step], self.orders[1][step])


def add_low(left, right):
    return (left.astype(F32) + right.astype(F32)).astype(BF)


def after(value, *others):
    return lax.optimization_barrier((value,) + others)[0]


class Chain:
    def __init__(self, links, walks, keep, send):
        self.links = links
        self.halvings = list(zip(*walks))
        self.whole = [(b, b) for b in range(CHUNK_BITS, links.bits)]
        self.doublings = list(zip(*[[d for d in reversed(w) if d != "y"] for w in walks]))
        self.keep = keep
        if isinstance(keep, tuple):
            high = links.swap(send[1], ("core", "core"))
            self.recv = (links.swap(send[0], ("core", "core")), high)
            self.at = 0
        else:
            self.recv = links.swap(send, self.halvings[0])
            self.at = 1

    def step(self, *others):
        keep, recv, links, at = self.keep, self.recv, self.links, self.at
        if others:
            keep = after(keep, *others) if at else (keep[0], after(keep[1], *others))
        self.at += 1
        if at == 0:
            send = add_low(keep[1], recv[1])
            self.keep = add_low(keep[0], recv[0])
            self.recv = links.swap(send, self.halvings[0])
            return send
        if at < len(self.halvings):
            half = keep.shape[0] // 2
            send = add_low(keep[half:], recv[half:])
            self.keep = add_low(after(keep, send)[:half], recv[:half])
            self.recv = links.swap(send, self.halvings[at])
            return send
        at -= len(self.halvings)
        if at <= len(self.whole):
            self.keep = add_low(keep, recv)
        else:
            self.keep = jnp.concatenate([keep, recv], axis=0)
        self.recv = links.swap(self.keep, (self.whole + self.doublings)[at])
        return self.keep

    def more(self):
        return self.at < len(self.halvings + self.whole + self.doublings)


def on_device(tokens, w_qkv, w_attn_out, w_in, w_down, gain_attn, gain_mlp, cotangent, *, n_dp, n_ctx):
    links = Links(n_dp, n_ctx)
    own, width = tokens.shape
    rows = w_qkv.shape[0]
    frows = w_down.shape[0]
    ff = frows * n_dp
    seq = own * n_ctx
    groups = width // 128
    step, fstep = rows // CHUNKS, frows // CHUNKS
    dp_at = lax.axis_index("dp")
    ctx_at = lax.axis_index("ctx")
    core = dp_at & 1
    upper = dp_at >> 1

    marks = []
    for walks in (FIRST_WALKS, SECOND_WALKS):
        both = []
        for walk in walks:
            bits = [b for b in walk if b != "y"]
            both.append(sum(((ctx_at >> b) & 1) << (CHUNK_BITS - 1 - i) for i, b in enumerate(bits)))
        marks += [jnp.where(core == 0, both[0], both[1]), jnp.where(core == 0, both[1], both[0])]
    z_at = (ctx_at >> 1) & 1
    svec = jnp.stack([dp_at, z_at, marks[0], marks[2], marks[3]]).astype(jnp.int32)

    half_rows = rows // 2
    near_sides = ("core", "core")

    def z_half(cols):
        return pl.BlockSpec((half_rows, cols), lambda i, s: (s[1], 0))

    qkv_y = links.swap(w_qkv, ("y", "y"))
    pair = jnp.concatenate([tokens, links.swap(tokens, links.both(links.bits - 1))], axis=0)
    qkv_c = links.swap(w_qkv, near_sides)
    gains = jnp.stack([gain_attn, gain_mlp]).astype(F32)
    gains_c = links.swap(gains, near_sides)
    gains_y = links.swap(gains, ("y", "y"))
    gains_cy = links.swap(gains_y, near_sides)

    flips = []
    for order in links.orders:
        at = np.arange(n_ctx)
        flips.append(sum(((at >> i) & 1) << order[links.bits - 1 - i] for i in range(links.bits)).astype(np.int32))
    owner = ctx_at ^ jnp.where(core == 0, jnp.asarray(flips[0]), jnp.asarray(flips[1]))
    owner = after(owner, pair)
    positions = (owner[:, None] * own + jnp.arange(own, dtype=jnp.int32)[None, :]).reshape(seq).astype(F32)
    half = HEAD_DIM // 2
    frequencies = jnp.exp(jnp.arange(half, dtype=F32) * (-2.0 * math.log(THETA) / HEAD_DIM))
    angles = positions[:, None] * frequencies[None, :]
    cos, sin = jnp.cos(angles), jnp.sin(angles)
    cos = jnp.concatenate([cos] * 4, axis=1)
    sin = jnp.concatenate([-sin, sin, -sin, sin], axis=1)

    half_up = pl.pallas_call(
        pack_up_kernel,
        grid_spec=pltpu.PrefetchScalarGridSpec(
            num_scalar_prefetch=1,
            grid=(1,),
            in_specs=[z_half(3 * width), z_half(width)],
            out_specs=whole((4 * half_rows, width)),
        ),
        out_shape=jax.ShapeDtypeStruct((4 * half_rows, width), BF),
        compiler_params=params(),
        cost_estimate=cost(COSTS["pack_up"]),
        name="pack_up",
    )(svec, after(w_in, cos, sin), w_attn_out)
    everyone = pair
    for i in reversed(range(1, links.bits - 1)):
        come = after(links.swap(everyone, links.both(i)), half_up, gains_y)
        everyone = jnp.concatenate([everyone, come], axis=0)
    far = links.swap(everyone, links.both(0))
    qkv_y = after(qkv_y, everyone)
    qkv_cy = links.swap(qkv_y, near_sides)
    up_first = links.swap(after(half_up, qkv_y), ("y", "y"))

    block = math.gcd(seq // 2, 256)
    turn = seq // 2 // block
    table = pl.BlockSpec((block, 128), lambda i, *_: (i, 0))
    rows_of = pl.BlockSpec((block, width), lambda i, *_: (i, 0))
    half_seq = jax.ShapeDtypeStruct((seq // 2, width), BF)
    normed_near, queries, keys_near, values_near, full_qkv, gains_full = pl.pallas_call(
        functools.partial(qkv_near_kernel, own=own),
        grid_spec=pltpu.PrefetchScalarGridSpec(
            num_scalar_prefetch=1,
            grid=(turn,),
            in_specs=[rows_of] + [whole(w_qkv.shape)] * 4 + [whole((2, rows))] * 4 + [table] * 2,
            out_specs=[rows_of, whole((own, width)), rows_of, rows_of, whole((width, 3 * width)), whole((2, width))],
        ),
        out_shape=[
            half_seq,
            jax.ShapeDtypeStruct((own, width), BF),
            half_seq,
            half_seq,
            jax.ShapeDtypeStruct((width, 3 * width), BF),
            jax.ShapeDtypeStruct((2, width), F32),
        ],
        compiler_params=params(),
        cost_estimate=cost(COSTS["qkv_near"]),
        name="qkv_near",
    )(svec, everyone, w_qkv, qkv_c, qkv_y, qkv_cy, gains, gains_c, gains_y, gains_cy, cos, sin)
    in_c, out_c, down_c = (links.swap(after(w, everyone), near_sides) for w in (w_in, w_attn_out, w_down))

    far_table = pl.BlockSpec((block, 128), lambda i, *_: (i + turn, 0))
    up_first = after(up_first, full_qkv)
    up_second = links.swap(up_first, (1, 1))
    down_y = links.swap(after(w_down, up_first), ("y", "y"))
    up_cf = links.swap(up_first, near_sides)
    normed_far, keys_far, values_far = pl.pallas_call(
        qkv_far_kernel,
        grid=(turn,),
        in_specs=[rows_of, pl.BlockSpec((width, 3 * width), lambda i: (0, 0)), whole((2, width)), far_table, far_table],
        out_specs=[rows_of] * 3,
        out_shape=[half_seq] * 3,
        compiler_params=params(),
        cost_estimate=cost(COSTS["qkv_far"]),
        name="qkv_far",
    )(after(far, up_first, in_c, out_c, down_c), full_qkv, gains_full, cos, sin)
    keys = (keys_near, keys_far)
    values = (values_near, values_far)

    own_pair = pl.BlockSpec((own, 128), lambda g: (0, g))
    seq_pair = pl.BlockSpec((seq, 128), lambda g: (0, g))
    half_pair = pl.BlockSpec((seq // 2, 128), lambda g: (0, g))
    turned_pair = pl.BlockSpec((128, own), lambda g: (g, 0))
    lse_pair = pl.BlockSpec((1, 8, own), lambda g: (g, 0, 0))
    attn_t, lse = pl.pallas_call(
        attend_kernel,
        grid=(groups,),
        in_specs=[own_pair] + [half_pair] * 4,
        out_specs=[turned_pair, lse_pair],
        out_shape=[jax.ShapeDtypeStruct((width, own), F32), jax.ShapeDtypeStruct((groups, 8, own), F32)],
        compiler_params=params(),
        cost_estimate=cost(COSTS["attend"]),
        name="attend",
    )(queries, *keys, *values)
    up_second = after(up_second, attn_t)
    down_y = after(down_y, attn_t)

    up_cs = links.swap(up_second, near_sides)
    down_cy = links.swap(down_y, near_sides)


    vm = pl.BlockSpec(memory_space=pltpu.VMEM)
    length = (4 * step + fstep) * width // 16
    part = 2 * rows + frows
    layer_out, d_mid, payload, d_attn_t, share_mine, share_core, share_y = pl.pallas_call(
        middle_kernel,
        in_specs=[pl.BlockSpec(memory_space=pltpu.SMEM)] + [vm] * 17,
        out_specs=[vm] * 7,
        out_shape=[
            jax.ShapeDtypeStruct((own, width), BF),
            jax.ShapeDtypeStruct((own, width), F32),
            jax.ShapeDtypeStruct((1, own + 16, width), BF),
            jax.ShapeDtypeStruct((width, own), BF),
            jax.ShapeDtypeStruct((part, own), BF),
            jax.ShapeDtypeStruct((part + 5 * width, own), BF),
            jax.ShapeDtypeStruct((2 * part + 5 * width, own), BF),
        ],
        scratch_shapes=[
            pltpu.VMEM((width, 3 * width), BF),
            pltpu.VMEM((width, width), BF),
            pltpu.VMEM((ff, width), BF),
            pltpu.VMEM((width, own), BF),
            pltpu.VMEM((width, own), BF),
            pltpu.VMEM((ff, own), BF),
        ],
        compiler_params=params(),
        cost_estimate=cost(COSTS["middle"]),
        name="middle",
    )(
        svec, tokens, attn_t, lse, w_in, in_c, w_attn_out, out_c, up_first, up_second, up_cf, up_cs,
        w_down, down_c, down_y, down_cy, cotangent, gains_full,
    )

    come_y = links.swap(share_y, ("y", "y"))
    come_c = links.swap(share_core, near_sides)

    d_query, d_kv = pl.pallas_call(
        attend_back_kernel,
        grid=(groups,),
        in_specs=[
            own_pair, half_pair, half_pair, half_pair, half_pair,
            pl.BlockSpec((1, own + 16, 128), lambda g: (0, 0, g)), turned_pair, turned_pair, lse_pair,
            whole((seq, 128)), whole((seq, 128)),
        ],
        out_specs=[own_pair, pl.BlockSpec((2, seq, 128), lambda g: (0, 0, g))],
        out_shape=[jax.ShapeDtypeStruct((own, width), BF), jax.ShapeDtypeStruct((2, seq, width), BF)],
        compiler_params=params(),
        cost_estimate=cost(COSTS["attend_back"]),
        name="attend_back",
    )(queries, *keys, *values, payload, d_attn_t, attn_t, lse, cos, sin)

    deep = math.gcd(seq // 2, 1024)
    turns = seq // 2 // deep
    second_parts = pl.pallas_call(
        qkv_grad_kernel,
        grid_spec=pltpu.PrefetchScalarGridSpec(
            num_scalar_prefetch=1,
            grid=(2 * turns,),
            in_specs=[
                pl.BlockSpec((deep, width), lambda i, s: (jnp.minimum(i, turns - 1), 0)),
                pl.BlockSpec((deep, width), lambda i, s: (jnp.maximum(i - turns, 0), 0)),
                pl.BlockSpec((2, deep, width), lambda i, s: (0, i, 0)),
                whole((own, width)),
            ],
            out_specs=[whole((CHUNKS, 16, step * 3 * width // 16))] * 4,
            scratch_shapes=[pltpu.VMEM((width, 3 * width), F32)],
        ),
        out_shape=[jax.ShapeDtypeStruct((CHUNKS, 16, step * 3 * width // 16), BF)] * 4,
        compiler_params=params(),
        cost_estimate=cost(COSTS["qkv_grad"]),
        name="qkv_grad",
    )(svec, normed_near, normed_far, d_kv, d_query)

    second = Chain(links, SECOND_WALKS, second_parts[:2], second_parts[2:])
    every_query = pl.pallas_call(
        queries_kernel,
        grid=(2 * turn,),
        in_specs=[
            pl.BlockSpec((block, width), lambda i: (jnp.minimum(i, turn - 1), 0)),
            pl.BlockSpec((block, width), lambda i: (jnp.maximum(i - turn, 0), 0)),
            pl.BlockSpec((width, width), lambda i: (0, 0)),
            table,
            table,
        ],
        out_specs=rows_of,
        out_shape=jax.ShapeDtypeStruct((seq, width), BF),
        compiler_params=params(),
        cost_estimate=cost(COSTS["every_query"]),
        name="every_query",
    )(after(normed_near, second_parts[0]), normed_far, full_qkv, cos, sin)
    come_y = after(come_y, every_query)
    come_cy = links.swap(come_y, near_sides)
    sent = second.step(come_y)
    first_low, first_high = pl.pallas_call(
        middle_grad_kernel,
        in_specs=[pl.BlockSpec(memory_space=pltpu.SMEM)] + [vm] * 5,
        out_specs=[vm] * 2,
        out_shape=[jax.ShapeDtypeStruct((CHUNKS // 2, 16, length), BF)] * 2,
        scratch_shapes=[
            pltpu.VMEM((part, n_dp * own), BF),
            pltpu.VMEM((n_dp * own, 5 * width), BF),
            pltpu.VMEM((rows, 3 * width), F32),
            pltpu.VMEM((rows, width), F32),
            pltpu.VMEM((frows, width), F32),
        ],
        compiler_params=params(),
        cost_estimate=cost(COSTS["middle_grad"]),
        name="middle_grad",
    )(svec, after(share_mine, sent), share_core, come_c, come_y, come_cy)
    first = Chain(links, FIRST_WALKS, first_low, first_high)
    gathered = links.swap(payload, links.both(links.bits - 1))
    gathered = jnp.concatenate([payload, after(gathered, first_high)], axis=0)
    late = first.step(second.step(first.step(second.step(gathered))))
    for i in reversed(range(1, links.bits - 1)):
        come = links.swap(gathered, links.both(i))
        gathered = jnp.concatenate([gathered, after(come, late)], axis=0)
    gathered_far = links.swap(gathered, links.both(0))
    late = second.step(first.step(gathered))

    d_key, d_value = pl.pallas_call(
        attend_keys_kernel,
        grid=(groups,),
        in_specs=[
            seq_pair, own_pair, own_pair,
            pl.BlockSpec((n_ctx // 2, own + 16, 128), lambda g: (0, 0, g)),
            pl.BlockSpec((n_ctx // 2, own + 16, 128), lambda g: (0, 0, g)),
            whole((own, 128)), whole((own, 128)),
        ],
        out_specs=[own_pair, own_pair],
        out_shape=[jax.ShapeDtypeStruct((own, width), BF)] * 2,
        compiler_params=params(),
        cost_estimate=cost(COSTS["attend_keys"]),
        name="attend_keys",
    )(every_query, keys_near, values_near, gathered, after(gathered_far, late), cos, sin)

    late = second.step(first.step(d_key))

    tokens_grad = pl.pallas_call(
        tokens_grad_kernel,
        in_specs=[vm] * 7,
        out_specs=vm,
        out_shape=jax.ShapeDtypeStruct((own, width), F32),
        compiler_params=params(),
        cost_estimate=cost(COSTS["tokens_grad"]),
        name="tokens_grad",
    )(after(tokens, late), d_query, d_key, d_value, full_qkv, gains_full, d_mid)
    late = tokens_grad
    while first.more() or second.more():
        for chain in (first, second):
            if chain.more():
                late = chain.step(late)

    def finish(chain, weight, shapes, mark, row, name):
        half = CHUNKS // 2
        done = ()
        for begin, part in ((0, chain.keep), (half, chain.recv)):

            def rows_at(count, cols, begin=begin):
                return pl.BlockSpec((count, cols), lambda i, s: ((i + begin) ^ s[mark], 0))

            big = [jax.ShapeDtypeStruct((r * CHUNKS, c), F32) for r, c in shapes]
            done = pl.pallas_call(
                functools.partial(finish_kernel, shapes=shapes, mark=mark, row=row, begin=begin),
                grid_spec=pltpu.PrefetchScalarGridSpec(
                    num_scalar_prefetch=1,
                    grid=(half,),
                    in_specs=[
                        pl.BlockSpec((1, 16, part.shape[2]), lambda i, s: (i, 0, 0)),
                        rows_at(*shapes[0]),
                        whole((2, rows)),
                    ]
                    + ([whole((1, rows))] + [pl.BlockSpec(memory_space=pl.ANY)] * len(shapes) if begin else []),
                    out_specs=[rows_at(*shape) for shape in shapes] + [whole((1, rows))],
                ),
                out_shape=big + [jax.ShapeDtypeStruct((1, rows), F32)],
                input_output_aliases={5 + i: i for i in range(len(shapes))} if begin else {},
                compiler_params=params(),
                cost_estimate=cost(COSTS[name]),
                name=name,
            )(svec, part, weight, gains, *((done[-1], *done[:-1]) if begin else ()))
        return done

    first_shapes = ((step, 3 * width), (step, width), (fstep, width))
    in_grad, out_grad, down_grad, gain_mlp_sum = finish(first, w_in, first_shapes, 2, 1, "finish_first")
    qkv_grad, gain_attn_sum = finish(second, w_qkv, ((step, 3 * width),), 3, 0, "finish_second")

    return (
        layer_out,
        tokens_grad,
        qkv_grad,
        out_grad,
        in_grad,
        down_grad,
        gain_attn_sum.reshape(rows),
        gain_mlp_sum.reshape(rows),
    )


def solution(mesh):
    return jax.shard_map(
        functools.partial(on_device, n_dp=mesh.shape["dp"], n_ctx=mesh.shape["ctx"]),
        mesh=mesh,
        in_specs=(
            P(("dp", "ctx"), None),
            P("dp", None),
            P("dp", None),
            P("dp", None),
            P("dp", None),
            P("dp"),
            P("dp"),
            P(("dp", "ctx"), None),
        ),
        out_specs=(
            P(("dp", "ctx"), None),
            P(("dp", "ctx"), None),
            P("dp", None),
            P("dp", None),
            P("dp", None),
            P("dp", None),
            P("dp"),
            P("dp"),
        ),
        check_vma=False,
    )
```

```python
import functools
import math

import jax
import jax.numpy as jnp
import numpy as np
from jax import lax
from jax.experimental import pallas as pl
from jax.experimental.pallas import tpu as pltpu
from jax.sharding import PartitionSpec as P

HEADS = 12
HEAD_DIM = 64
THETA = 160000.0
EPS = 1e-05
CHUNK_BITS = 2
CHUNKS = 1 << CHUNK_BITS
BF = jnp.bfloat16
F32 = jnp.float32
COSTS = {
    "pack_up": 0.5,
    "qkv_near": 0.5,
    "qkv_far": 0.5,
    "attend": 0.5,
    "middle": 0.5,
    "middle_grad": 0.5,
    "every_query": 0.5,
    "attend_back": 0.5,
    "qkv_grad": 0.5,
    "attend_keys": 0.5,
    "tokens_grad": 0.5,
    "finish_first": 0.5,
    "finish_second": 0.5,
}
FIRST_WALKS = ((0, 1), (1, 0))
SECOND_WALKS = (("y", 0, 1), (1, "y", 0))
VMEM = {
    "pack_up": 8,
    "qkv_near": 26,
    "qkv_far": 26,
    "attend": 12,
    "middle": 26,
    "middle_grad": 26,
    "every_query": 16,
    "attend_back": 20,
    "qkv_grad": 26,
    "attend_keys": 20,
    "tokens_grad": 16,
    "finish_first": 12,
    "finish_second": 12,
}
VMEM_LONG = 58
SHORT = 1024


def whole(shape):
    return pl.BlockSpec(shape, lambda *_: (0,) * len(shape))


def cost(micros):
    return pl.CostEstimate(flops=int(micros * 1.15e9), bytes_accessed=0, transcendentals=0)


def dot(left, right, dims=((1,), (0,))):
    return lax.dot_general(left, right, (dims, ((), ())), preferred_element_type=F32)


NT = ((1,), (1,))
TN = ((0,), (0,))


def normalise(values):
    center = values - jnp.mean(values, axis=-1, keepdims=True)
    spread = jnp.mean(center * center, axis=-1, keepdims=True)
    scale = lax.rsqrt(spread + EPS)
    return center * scale, scale


def norm_back(grad, xhat, scale, gain):
    inner = grad * gain
    return scale * (
        inner
        - jnp.mean(inner, axis=-1, keepdims=True)
        - xhat * jnp.mean(inner * xhat, axis=-1, keepdims=True)
    )


def swap_halves(values):
    lane = lax.broadcasted_iota(jnp.int32, values.shape, 1)
    return jnp.where(lane % 64 < 32, pltpu.roll(values, 96, 1), pltpu.roll(values, 32, 1))


def rotate(values, cos, sin):
    return values * cos + swap_halves(values) * sin


def rotate_back(values, cos, sin):
    return values * cos - swap_halves(values) * sin


def fold(pieces):
    rows = [p[8 * i : 8 * i + 8] for p in pieces for i in range(p.shape[0] // 8)]
    flat = jnp.concatenate(rows, axis=1)
    half = flat.shape[1] // 2
    return jnp.concatenate([flat[:, :half], flat[:, half:]], axis=0)


def unfold(block, shapes):
    flat = jnp.concatenate([block[:8], block[8:]], axis=1)
    out, at = [], 0
    for rows, cols in shapes:
        parts = []
        for _ in range(rows // 8):
            parts.append(flat[:, at : at + cols])
            at += cols
        out.append(jnp.concatenate(parts, axis=0))
    return out


def chunk_at(svec, keep, spot):
    found = []
    for walk in SECOND_WALKS:
        low = CHUNK_BITS - walk.index("y")
        rel = ((spot >> (low + 1)) << low) | (spot & ((1 << low) - 1))
        found.append(((spot >> low) & 1, rel))
    core = (svec[0] & 1) ^ keep
    upper = jnp.where(core == 0, found[0][0], found[1][0])
    return upper, jnp.where(core == 0, found[0][1], found[1][1]) ^ svec[3 + keep]


def spread(svec, pieces, half, begins, to_ref, to_cols):
    for j, parts in enumerate(pieces):
        halved = len(parts) == 3
        for h in range(2):
            to = (svec[0] ^ j) * (2 * half) + (svec[1] ^ h if halved else h) * half
            at = begins[1] if halved else begins[0] + h * half
            part = parts[h if halved else 0]
            to_ref[pl.ds(pl.multiple_of(to, 16), half), to_cols] = part[at : at + half, parts[-1]]


def pack_up_kernel(svec, in_ref, w_ref, out_ref):
    half, width = w_ref.shape
    for b in range(3):
        out_ref[b * half : (b + 1) * half, :] = in_ref[:, b * width : (b + 1) * width]
    out_ref[3 * half :, :] = w_ref[...]


def project(x_ref, gain, cos_ref, sin_ref, w_ref, n_ref, k_ref, v_ref):
    width = n_ref.shape[1]
    xhat, _ = normalise(x_ref[...].astype(F32))
    normed = (xhat * gain).astype(BF)
    n_ref[...] = normed
    cos, sin = cos_ref[...], sin_ref[...]
    keys = dot(normed, w_ref[:, width : 2 * width])
    for g in range(width // 128):
        cut = slice(128 * g, 128 * g + 128)
        k_ref[:, cut] = rotate(keys[:, cut], cos, sin).astype(BF)
    v_ref[...] = dot(normed, w_ref[:, 2 * width :]).astype(BF)
    return normed, cos, sin


def qkv_near_kernel(
    svec, x_ref, w0, w1, w2, w3, g0_ref, g1_ref, g2_ref, g3_ref, cos_ref, sin_ref,
    n_ref, q_ref, k_ref, v_ref, w_ref, gain_ref, *, own,
):
    rows = w_ref.shape[0] // 4
    width = n_ref.shape[1]
    first = pl.program_id(0) == 0

    @pl.when(first)
    def _():
        for j, piece in enumerate((w0, w1, w2, w3)):
            w_ref[pl.ds(pl.multiple_of((svec[0] ^ j) * rows, 16), rows), :] = piece[...]
        g = [r[:, :rows] for r in (g0_ref, g1_ref, g2_ref, g3_ref)]
        core, upper = svec[0] & 1, svec[0] >> 1
        near = jnp.where(core == 0, jnp.concatenate([g[0], g[1]], axis=1), jnp.concatenate([g[1], g[0]], axis=1))
        far = jnp.where(core == 0, jnp.concatenate([g[2], g[3]], axis=1), jnp.concatenate([g[3], g[2]], axis=1))
        full = jnp.where(upper == 0, jnp.concatenate([near, far], axis=1), jnp.concatenate([far, near], axis=1))
        gain_ref[...] = full

    normed, cos, sin = project(x_ref, gain_ref[0:1, :], cos_ref, sin_ref, w_ref, n_ref, k_ref, v_ref)

    @pl.when(first)
    def _():
        queries = dot(normed[:own], w_ref[:, :width])
        for g in range(width // 128):
            cut = slice(128 * g, 128 * g + 128)
            q_ref[:, cut] = rotate(queries[:, cut], cos[:own], sin[:own]).astype(BF)


def qkv_far_kernel(x_ref, w_ref, gain_ref, cos_ref, sin_ref, n_ref, k_ref, v_ref):
    project(x_ref, gain_ref[0:1, :], cos_ref, sin_ref, w_ref, n_ref, k_ref, v_ref)


def both_halves(near_ref, far_ref):
    return jnp.concatenate([near_ref[...], far_ref[...]], axis=0)


def queries_kernel(near_ref, far_ref, w_ref, cos_ref, sin_ref, q_ref):
    there = pl.program_id(0) >= pl.num_programs(0) // 2
    queries = dot(jnp.where(there, far_ref[...], near_ref[...]), w_ref[...])
    cos, sin = cos_ref[...], sin_ref[...]
    for g in range(queries.shape[1] // 128):
        cut = slice(128 * g, 128 * g + 128)
        q_ref[:, cut] = rotate(queries[:, cut], cos, sin).astype(BF)


def head_mask(shape, head):
    return lax.broadcasted_iota(jnp.int32, shape, 1) // HEAD_DIM == head


def fold_scale(q, head):
    return jnp.where(head_mask(q.shape, head), q, jnp.zeros_like(q)) * jnp.asarray(HEAD_DIM**-0.5, BF)


def attend_kernel(q_ref, kn_ref, kf_ref, vn_ref, vf_ref, o_ref, lse_ref):
    q, k, v = q_ref[...], both_halves(kn_ref, kf_ref), both_halves(vn_ref, vf_ref)
    for h in range(2):
        scores = dot(k, fold_scale(q, h), NT)
        top = jnp.max(scores, axis=0, keepdims=True)
        weights = jnp.exp(scores - top)
        total = jnp.sum(weights, axis=0, keepdims=True)
        out = dot(v, weights.astype(BF), TN)
        cut = slice(HEAD_DIM * h, HEAD_DIM * h + HEAD_DIM)
        o_ref[cut, :] = out[cut, :] / total
        lse_ref[0, h : h + 1, :] = top + jnp.log(total)


def middle_kernel(
    svec, x_ref, at_ref, lse_ref, i0, i1, o0, o1, af, as_, acf, acs, b0, b1, b2, b3, dy_ref, gains_ref,
    lo_ref, dm_ref, pay_ref, dat_ref, mine_ref, core_ref, y_ref,
    win, wout, wdown, n2t, attnt, hidt,
):
    width = x_ref.shape[1]
    own = x_ref.shape[0]
    half = width // 8
    ff = wdown.shape[0]
    frows = ff // 4
    every = slice(None)
    for b in range(3):
        cut = slice(b * width, (b + 1) * width)
        spread(svec, ((i0, cut), (i1, cut), (af, as_, every), (acf, acs, every)), half, (0, b * half), win, cut)
    spread(svec, ((o0, every), (o1, every), (af, as_, every), (acf, acs, every)), half, (0, 3 * half), wout, every)
    for j, piece in enumerate((b0, b1, b2, b3)):
        wdown[pl.ds(pl.multiple_of((svec[0] ^ j) * frows, 16), frows), :] = piece[...]

    gain = gains_ref[1:2, :]
    attn_t = at_ref[...]
    attnt[...] = attn_t.astype(BF)
    attn_low = jnp.transpose(attn_t).astype(BF)
    mid = x_ref[...].astype(F32) + dot(attn_low, wout[...])
    xhat, scale = normalise(mid)
    normed = xhat * gain
    n2t[...] = jnp.transpose(normed).astype(BF)
    up = dot(normed.astype(BF), win[...])
    gate, lin = up[:, :ff], up[:, ff:]
    cdf = 0.5 * (1.0 + lax.erf(gate * (2.0**-0.5)))
    act = gate * cdf
    hidden = act * lin
    hidt[...] = jnp.transpose(hidden).astype(BF)
    lo_ref[...] = (mid + dot(hidden.astype(BF), wdown[...])).astype(BF)
    dy = dy_ref[...]
    d_hidden = dot(dy, wdown[...], NT)
    pdf = jnp.exp(-0.5 * gate * gate) * (1.0 / math.sqrt(2.0 * math.pi))
    d_gate = (d_hidden * lin * (cdf + gate * pdf)).astype(BF)
    d_lin = (d_hidden * act).astype(BF)
    d_up = jnp.concatenate([d_gate, d_lin], axis=1)
    d_mid = dy.astype(F32) + norm_back(dot(d_up, win[...], NT), xhat, scale, gain)
    dm_ref[...] = d_mid
    d_branch = d_mid.astype(BF)
    rows = width // 4
    part = 2 * rows + frows
    for j, (to_ref, begin) in enumerate(((mine_ref, 0), (core_ref, 0), (y_ref, 0), (y_ref, part))):
        q = svec[0] ^ j
        at = pl.multiple_of(q * rows, 16)
        to_ref[begin : begin + rows, :] = n2t[pl.ds(at, rows), :]
        to_ref[begin + rows : begin + 2 * rows, :] = attnt[pl.ds(at, rows), :]
        to_ref[begin + 2 * rows : begin + part, :] = hidt[pl.ds(pl.multiple_of(q * frows, 16), frows), :]
    d_all = jnp.concatenate([d_up, d_branch, dy], axis=1)
    for b in range(5 * width // 128):
        piece = d_all[:, 128 * b : 128 * b + 128]
        for to_ref, begin in ((core_ref, part), (y_ref, 2 * part)):
            to_ref[begin + b * own : begin + (b + 1) * own, :] = piece
    pay_ref[0, :own, :] = dot(d_branch, wout[...], NT).astype(BF)
    d_attn_t = dot(wout[...], d_branch, NT).astype(BF)
    dat_ref[...] = d_attn_t
    prod = d_attn_t.astype(F32) * attn_t
    for g in range(width // 128):
        stats = []
        for h in range(2):
            begin = 128 * g + HEAD_DIM * h
            delta = jnp.sum(prod[begin : begin + HEAD_DIM, :], axis=0, keepdims=True)
            for row in (lse_ref[g, h : h + 1, :], delta):
                high = row.astype(BF).astype(F32)
                stats += [high, row - high]
        stats = jnp.concatenate(stats + [jnp.zeros((8, own), F32)], axis=0)
        pay_ref[0, own:, 128 * g : 128 * g + 128] = stats.astype(BF)


def middle_grad_kernel(
    svec, mine_ref, core_ref, c_ref, y_ref, cy_ref,
    low_ref, high_ref, left, right, g_in, g_out, g_down,
):
    part = mine_ref.shape[0]
    own = mine_ref.shape[1]
    width = right.shape[1] // 5
    rows = width // 4
    frows = part - 2 * rows
    step, fstep = rows // CHUNKS, frows // CHUNKS
    sources = ((mine_ref, 0, core_ref, part), (c_ref, 0, c_ref, part), (y_ref, 0, y_ref, 2 * part), (cy_ref, part, cy_ref, 2 * part))
    for i, (x_ref, x_at, d_ref, d_at) in enumerate(sources):
        left[:, i * own : (i + 1) * own] = x_ref[x_at : x_at + part, :]
        for b in range(5 * width // 128):
            right[i * own : (i + 1) * own, 128 * b : 128 * b + 128] = d_ref[d_at + b * own : d_at + (b + 1) * own, :]
    g_in[...] = dot(left[:rows, :], right[:, : 3 * width])
    g_out[...] = dot(left[rows : 2 * rows, :], right[:, 3 * width : 4 * width])
    g_down[...] = dot(left[2 * rows :, :], right[:, 4 * width :])
    for spot in reversed(range(CHUNKS)):
        c = spot ^ svec[2]
        at = pl.multiple_of(c * step, 8)
        fat = pl.multiple_of(c * fstep, 8)
        parts = [g_in[pl.ds(at, step), :], g_out[pl.ds(at, step), :], g_down[pl.ds(fat, fstep), :]]
        target = high_ref if spot >= CHUNKS // 2 else low_ref
        target[spot % (CHUNKS // 2)] = fold(parts).astype(BF)


def attend_back_kernel(q_ref, kn_ref, kf_ref, vn_ref, vf_ref, da_ref, dat_ref, at_ref, lse_ref, cos_ref, sin_ref, dq_ref, dkv_ref):
    q, k, v = q_ref[...], both_halves(kn_ref, kf_ref), both_halves(vn_ref, vf_ref)
    own = q.shape[0]
    da = da_ref[0, :own, :]
    prod = dat_ref[...].astype(F32) * at_ref[...]
    d_key, d_value, d_query = 0.0, 0.0, []
    for h in range(2):
        cut = slice(HEAD_DIM * h, HEAD_DIM * h + HEAD_DIM)
        q_scaled = fold_scale(q, h)
        da_head = jnp.where(head_mask(da.shape, h), da, jnp.zeros_like(da))
        probs = jnp.exp(dot(k, q_scaled, NT) - lse_ref[0, h : h + 1, :])
        delta = jnp.sum(prod[cut, :], axis=0, keepdims=True)
        d_scores = (probs * (dot(v, da_head, NT) - delta)).astype(BF)
        d_value += dot(probs.astype(BF), da_head)
        d_key += dot(d_scores, q_scaled)
        d_query.append(dot(d_scores, k, TN))
    dkv_ref[0] = rotate_back(d_key, cos_ref[...], sin_ref[...]).astype(BF)
    dkv_ref[1] = d_value.astype(BF)
    d_q = jnp.where(head_mask(q.shape, 0), d_query[0], d_query[1]) * (HEAD_DIM**-0.5)
    dq_ref[...] = rotate_back(d_q, cos_ref[:own, :], sin_ref[:own, :]).astype(BF)


def attend_keys_kernel(q_ref, k_ref, v_ref, near_ref, far_ref, cos_ref, sin_ref, dk_ref, dv_ref):
    k, v, q = k_ref[...], v_ref[...], q_ref[...]
    own = k.shape[0]
    both = [(r, i) for r in (near_ref, far_ref) for i in range(near_ref.shape[0])]
    da = jnp.concatenate([r[i, :own, :] for r, i in both], axis=0)
    stats = jnp.concatenate([r[i, own:, :].astype(F32) for r, i in both], axis=1)
    d_key, d_value = [], []
    for h in range(2):
        lse = stats[4 * h : 4 * h + 1] + stats[4 * h + 1 : 4 * h + 2]
        delta = stats[4 * h + 2 : 4 * h + 3] + stats[4 * h + 3 : 4 * h + 4]
        v_head = jnp.where(head_mask(v.shape, h), v, jnp.zeros_like(v))
        probs = jnp.exp(dot(fold_scale(k, h), q, NT) - lse)
        d_scores = (probs * (dot(v_head, da, NT) - delta)).astype(BF)
        d_value.append(dot(probs.astype(BF), da))
        d_key.append(dot(d_scores, q))
    first = head_mask(k.shape, 0)
    d_k = jnp.where(first, d_key[0], d_key[1]) * (HEAD_DIM**-0.5)
    dk_ref[...] = rotate_back(d_k, cos_ref[...], sin_ref[...]).astype(BF)
    dv_ref[...] = jnp.where(first, d_value[0], d_value[1]).astype(BF)


def qkv_grad_kernel(svec, near_ref, far_ref, dkv_ref, dq_ref, keep_low, keep_high, send_low, send_high, acc):
    width = near_ref.shape[1]
    rows = width // 4
    step = rows // CHUNKS
    own = dq_ref.shape[0]
    at = pl.program_id(0)
    normed = jnp.where(at >= pl.num_programs(0) // 2, far_ref[...], near_ref[...])
    first = at == 0

    @pl.when(first)
    def _():
        acc[:, :width] = dot(normed[:own], dq_ref[...], TN)
        for b in range(2):
            acc[:, (b + 1) * width : (b + 2) * width] = dot(normed, dkv_ref[b], TN)

    @pl.when(jnp.logical_not(first))
    def _():
        for b in range(2):
            acc[:, (b + 1) * width : (b + 2) * width] += dot(normed, dkv_ref[b], TN)

    @pl.when(pl.program_id(0) == pl.num_programs(0) - 1)
    def _():
        for keep, low_ref, high_ref in ((1, send_low, send_high), (0, keep_low, keep_high)):
            for spot in range(2 * CHUNKS):
                u, c = chunk_at(svec, keep, spot)
                at = pl.multiple_of((svec[0] ^ (2 * u + keep)) * rows + c * step, 8)
                target = high_ref if spot >= CHUNKS else low_ref
                target[spot % CHUNKS] = fold([acc[pl.ds(at, step), :]]).astype(BF)


def tokens_grad_kernel(x_ref, dq_ref, dk_ref, dv_ref, w_ref, gains_ref, dm_ref, out_ref):
    d_proj = jnp.concatenate([dq_ref[...], dk_ref[...], dv_ref[...]], axis=1)
    d_normed = dot(d_proj, w_ref[...], NT)
    xhat, scale = normalise(x_ref[...].astype(F32))
    out_ref[...] = dm_ref[...] + norm_back(d_normed, xhat, scale, gains_ref[0:1, :])


def gain_rows(product, gain, chunk, before, gain_ref):
    rows, cols = product.shape[0], gain_ref.shape[1]
    total = jnp.sum(product, axis=1, keepdims=True)
    row = lax.broadcasted_iota(jnp.int32, (rows, cols), 0)
    col = lax.broadcasted_iota(jnp.int32, (rows, cols), 1)
    part = jnp.sum(jnp.where(col == row + chunk * rows, total, 0.0), axis=0, keepdims=True) / gain
    first = pl.program_id(0) == 0

    @pl.when(first)
    def _():
        gain_ref[...] = part + before

    @pl.when(jnp.logical_not(first))
    def _():
        gain_ref[...] += part


def finish_kernel(svec, part_ref, w_ref, own_gain, *refs, shapes, mark, row, begin):
    grads = unfold(part_ref[0].astype(F32), shapes)
    outs = refs[1 + len(shapes) :] if begin else refs
    for out_ref, grad in zip(outs, grads):
        out_ref[...] = grad
    before = refs[0][...] if begin else 0.0
    chunk = (pl.program_id(0) + begin) ^ svec[mark]
    gain_rows(w_ref[...].astype(F32) * grads[0], own_gain[row : row + 1, :], chunk, before, outs[-1])


class Links:
    def __init__(self, n_dp, n_ctx):
        self.n_dp, self.n_ctx = n_dp, n_ctx
        self.bits = n_ctx.bit_length() - 1
        rise = list(range(self.bits))
        self.orders = (rise, rise[1:] + rise[:1])

    def swap(self, value, dims):
        pairs = []
        for d in range(self.n_dp):
            dim = dims[d & 1]
            for c in range(self.n_ctx):
                if dim == "core":
                    to = (d ^ 1, c)
                elif dim == "y":
                    to = (d ^ 2, c)
                else:
                    to = (d, c ^ (1 << dim))
                pairs.append((d * self.n_ctx + c, to[0] * self.n_ctx + to[1]))
        return lax.ppermute(value, ("dp", "ctx"), pairs)

    def both(self, step):
        return (self.orders[0][step], self.orders[1][step])


def add_low(left, right):
    return (left.astype(F32) + right.astype(F32)).astype(BF)


def after(value, *others):
    return lax.optimization_barrier((value,) + others)[0]


class Chain:
    def __init__(self, links, walks, keep, send):
        self.links = links
        self.halvings = list(zip(*walks))
        self.whole = [(b, b) for b in range(CHUNK_BITS, links.bits)]
        self.doublings = list(zip(*[[d for d in reversed(w) if d != "y"] for w in walks]))
        self.keep = keep
        if isinstance(keep, tuple):
            high = links.swap(send[1], ("core", "core"))
            self.recv = (links.swap(send[0], ("core", "core")), high)
            self.at = 0
        else:
            self.recv = links.swap(send, self.halvings[0])
            self.at = 1

    def step(self, *others):
        keep, recv, links, at = self.keep, self.recv, self.links, self.at
        if others:
            keep = after(keep, *others) if at else (keep[0], after(keep[1], *others))
        self.at += 1
        if at == 0:
            send = add_low(keep[1], recv[1])
            self.keep = add_low(keep[0], recv[0])
            self.recv = links.swap(send, self.halvings[0])
            return send
        if at < len(self.halvings):
            half = keep.shape[0] // 2
            send = add_low(keep[half:], recv[half:])
            self.keep = add_low(after(keep, send)[:half], recv[:half])
            self.recv = links.swap(send, self.halvings[at])
            return send
        at -= len(self.halvings)
        if at <= len(self.whole):
            self.keep = add_low(keep, recv)
        else:
            self.keep = jnp.concatenate([keep, recv], axis=0)
        self.recv = links.swap(self.keep, (self.whole + self.doublings)[at])
        return self.keep

    def more(self):
        return self.at < len(self.halvings + self.whole + self.doublings)


def on_device(tokens, w_qkv, w_attn_out, w_in, w_down, gain_attn, gain_mlp, cotangent, *, n_dp, n_ctx):
    links = Links(n_dp, n_ctx)
    own, width = tokens.shape
    rows = w_qkv.shape[0]
    frows = w_down.shape[0]
    ff = frows * n_dp
    seq = own * n_ctx
    groups = width // 128

    def room(name):
        size = VMEM[name] if seq <= SHORT else VMEM_LONG
        return pltpu.CompilerParams(vmem_limit_bytes=size * 1024 * 1024)

    step, fstep = rows // CHUNKS, frows // CHUNKS
    dp_at = lax.axis_index("dp")
    ctx_at = lax.axis_index("ctx")
    core = dp_at & 1
    upper = dp_at >> 1

    marks = []
    for walks in (FIRST_WALKS, SECOND_WALKS):
        both = []
        for walk in walks:
            bits = [b for b in walk if b != "y"]
            both.append(sum(((ctx_at >> b) & 1) << (CHUNK_BITS - 1 - i) for i, b in enumerate(bits)))
        marks += [jnp.where(core == 0, both[0], both[1]), jnp.where(core == 0, both[1], both[0])]
    z_at = (ctx_at >> 1) & 1
    svec = jnp.stack([dp_at, z_at, marks[0], marks[2], marks[3]]).astype(jnp.int32)

    half_rows = rows // 2
    near_sides = ("core", "core")

    def z_half(cols):
        return pl.BlockSpec((half_rows, cols), lambda i, s: (s[1], 0))

    qkv_y = links.swap(w_qkv, ("y", "y"))
    pair = jnp.concatenate([tokens, links.swap(tokens, links.both(links.bits - 1))], axis=0)
    qkv_c = links.swap(w_qkv, near_sides)
    gains = jnp.stack([gain_attn, gain_mlp]).astype(F32)
    gains_c = links.swap(gains, near_sides)
    gains_y = links.swap(gains, ("y", "y"))
    gains_cy = links.swap(gains_y, near_sides)

    flips = []
    for order in links.orders:
        at = np.arange(n_ctx)
        flips.append(sum(((at >> i) & 1) << order[links.bits - 1 - i] for i in range(links.bits)).astype(np.int32))
    owner = ctx_at ^ jnp.where(core == 0, jnp.asarray(flips[0]), jnp.asarray(flips[1]))
    owner = after(owner, pair)
    positions = (owner[:, None] * own + jnp.arange(own, dtype=jnp.int32)[None, :]).reshape(seq).astype(F32)
    half = HEAD_DIM // 2
    frequencies = jnp.exp(jnp.arange(half, dtype=F32) * (-2.0 * math.log(THETA) / HEAD_DIM))
    angles = positions[:, None] * frequencies[None, :]
    cos, sin = jnp.cos(angles), jnp.sin(angles)
    cos = jnp.concatenate([cos] * 4, axis=1)
    sin = jnp.concatenate([-sin, sin, -sin, sin], axis=1)

    half_up = pl.pallas_call(
        pack_up_kernel,
        grid_spec=pltpu.PrefetchScalarGridSpec(
            num_scalar_prefetch=1,
            grid=(1,),
            in_specs=[z_half(3 * width), z_half(width)],
            out_specs=whole((4 * half_rows, width)),
        ),
        out_shape=jax.ShapeDtypeStruct((4 * half_rows, width), BF),
        compiler_params=room("pack_up"),
        cost_estimate=cost(COSTS["pack_up"]),
        name="pack_up",
    )(svec, after(w_in, cos, sin), w_attn_out)
    everyone = pair
    for i in reversed(range(1, links.bits - 1)):
        come = after(links.swap(everyone, links.both(i)), half_up, gains_y)
        everyone = jnp.concatenate([everyone, come], axis=0)
    far = links.swap(everyone, links.both(0))
    qkv_y = after(qkv_y, everyone)
    qkv_cy = links.swap(qkv_y, near_sides)
    up_first = links.swap(after(half_up, qkv_y), ("y", "y"))

    block = math.gcd(seq // 2, 256)
    turn = seq // 2 // block
    table = pl.BlockSpec((block, 128), lambda i, *_: (i, 0))
    rows_of = pl.BlockSpec((block, width), lambda i, *_: (i, 0))
    half_seq = jax.ShapeDtypeStruct((seq // 2, width), BF)
    normed_near, queries, keys_near, values_near, full_qkv, gains_full = pl.pallas_call(
        functools.partial(qkv_near_kernel, own=own),
        grid_spec=pltpu.PrefetchScalarGridSpec(
            num_scalar_prefetch=1,
            grid=(turn,),
            in_specs=[rows_of] + [whole(w_qkv.shape)] * 4 + [whole((2, rows))] * 4 + [table] * 2,
            out_specs=[rows_of, whole((own, width)), rows_of, rows_of, whole((width, 3 * width)), whole((2, width))],
        ),
        out_shape=[
            half_seq,
            jax.ShapeDtypeStruct((own, width), BF),
            half_seq,
            half_seq,
            jax.ShapeDtypeStruct((width, 3 * width), BF),
            jax.ShapeDtypeStruct((2, width), F32),
        ],
        compiler_params=room("qkv_near"),
        cost_estimate=cost(COSTS["qkv_near"]),
        name="qkv_near",
    )(svec, everyone, w_qkv, qkv_c, qkv_y, qkv_cy, gains, gains_c, gains_y, gains_cy, cos, sin)
    in_c, out_c, down_c = (links.swap(after(w, everyone), near_sides) for w in (w_in, w_attn_out, w_down))

    far_table = pl.BlockSpec((block, 128), lambda i, *_: (i + turn, 0))
    up_first = after(up_first, full_qkv)
    up_second = links.swap(up_first, (1, 1))
    down_y = links.swap(after(w_down, up_first), ("y", "y"))
    up_cf = links.swap(up_first, near_sides)
    normed_far, keys_far, values_far = pl.pallas_call(
        qkv_far_kernel,
        grid=(turn,),
        in_specs=[rows_of, pl.BlockSpec((width, 3 * width), lambda i: (0, 0)), whole((2, width)), far_table, far_table],
        out_specs=[rows_of] * 3,
        out_shape=[half_seq] * 3,
        compiler_params=room("qkv_far"),
        cost_estimate=cost(COSTS["qkv_far"]),
        name="qkv_far",
    )(after(far, up_first, in_c, out_c, down_c), full_qkv, gains_full, cos, sin)
    keys = (keys_near, keys_far)
    values = (values_near, values_far)

    own_pair = pl.BlockSpec((own, 128), lambda g: (0, g))
    seq_pair = pl.BlockSpec((seq, 128), lambda g: (0, g))
    half_pair = pl.BlockSpec((seq // 2, 128), lambda g: (0, g))
    turned_pair = pl.BlockSpec((128, own), lambda g: (g, 0))
    lse_pair = pl.BlockSpec((1, 8, own), lambda g: (g, 0, 0))
    attn_t, lse = pl.pallas_call(
        attend_kernel,
        grid=(groups,),
        in_specs=[own_pair] + [half_pair] * 4,
        out_specs=[turned_pair, lse_pair],
        out_shape=[jax.ShapeDtypeStruct((width, own), F32), jax.ShapeDtypeStruct((groups, 8, own), F32)],
        compiler_params=room("attend"),
        cost_estimate=cost(COSTS["attend"]),
        name="attend",
    )(queries, *keys, *values)
    up_second = after(up_second, attn_t)
    down_y = after(down_y, attn_t)

    up_cs = links.swap(up_second, near_sides)
    down_cy = links.swap(down_y, near_sides)


    vm = pl.BlockSpec(memory_space=pltpu.VMEM)
    length = (4 * step + fstep) * width // 16
    part = 2 * rows + frows
    layer_out, d_mid, payload, d_attn_t, share_mine, share_core, share_y = pl.pallas_call(
        middle_kernel,
        in_specs=[pl.BlockSpec(memory_space=pltpu.SMEM)] + [vm] * 17,
        out_specs=[vm] * 7,
        out_shape=[
            jax.ShapeDtypeStruct((own, width), BF),
            jax.ShapeDtypeStruct((own, width), F32),
            jax.ShapeDtypeStruct((1, own + 16, width), BF),
            jax.ShapeDtypeStruct((width, own), BF),
            jax.ShapeDtypeStruct((part, own), BF),
            jax.ShapeDtypeStruct((part + 5 * width, own), BF),
            jax.ShapeDtypeStruct((2 * part + 5 * width, own), BF),
        ],
        scratch_shapes=[
            pltpu.VMEM((width, 3 * width), BF),
            pltpu.VMEM((width, width), BF),
            pltpu.VMEM((ff, width), BF),
            pltpu.VMEM((width, own), BF),
            pltpu.VMEM((width, own), BF),
            pltpu.VMEM((ff, own), BF),
        ],
        compiler_params=room("middle"),
        cost_estimate=cost(COSTS["middle"]),
        name="middle",
    )(
        svec, tokens, attn_t, lse, w_in, in_c, w_attn_out, out_c, up_first, up_second, up_cf, up_cs,
        w_down, down_c, down_y, down_cy, cotangent, gains_full,
    )

    come_y = links.swap(share_y, ("y", "y"))
    come_c = links.swap(share_core, near_sides)

    d_query, d_kv = pl.pallas_call(
        attend_back_kernel,
        grid=(groups,),
        in_specs=[
            own_pair, half_pair, half_pair, half_pair, half_pair,
            pl.BlockSpec((1, own + 16, 128), lambda g: (0, 0, g)), turned_pair, turned_pair, lse_pair,
            whole((seq, 128)), whole((seq, 128)),
        ],
        out_specs=[own_pair, pl.BlockSpec((2, seq, 128), lambda g: (0, 0, g))],
        out_shape=[jax.ShapeDtypeStruct((own, width), BF), jax.ShapeDtypeStruct((2, seq, width), BF)],
        compiler_params=room("attend_back"),
        cost_estimate=cost(COSTS["attend_back"]),
        name="attend_back",
    )(queries, *keys, *values, payload, d_attn_t, attn_t, lse, cos, sin)

    deep = math.gcd(seq // 2, 1024)
    turns = seq // 2 // deep
    second_parts = pl.pallas_call(
        qkv_grad_kernel,
        grid_spec=pltpu.PrefetchScalarGridSpec(
            num_scalar_prefetch=1,
            grid=(2 * turns,),
            in_specs=[
                pl.BlockSpec((deep, width), lambda i, s: (jnp.minimum(i, turns - 1), 0)),
                pl.BlockSpec((deep, width), lambda i, s: (jnp.maximum(i - turns, 0), 0)),
                pl.BlockSpec((2, deep, width), lambda i, s: (0, i, 0)),
                whole((own, width)),
            ],
            out_specs=[whole((CHUNKS, 16, step * 3 * width // 16))] * 4,
            scratch_shapes=[pltpu.VMEM((width, 3 * width), F32)],
        ),
        out_shape=[jax.ShapeDtypeStruct((CHUNKS, 16, step * 3 * width // 16), BF)] * 4,
        compiler_params=room("qkv_grad"),
        cost_estimate=cost(COSTS["qkv_grad"]),
        name="qkv_grad",
    )(svec, normed_near, normed_far, d_kv, d_query)

    second = Chain(links, SECOND_WALKS, second_parts[:2], second_parts[2:])
    every_query = pl.pallas_call(
        queries_kernel,
        grid=(2 * turn,),
        in_specs=[
            pl.BlockSpec((block, width), lambda i: (jnp.minimum(i, turn - 1), 0)),
            pl.BlockSpec((block, width), lambda i: (jnp.maximum(i - turn, 0), 0)),
            pl.BlockSpec((width, width), lambda i: (0, 0)),
            table,
            table,
        ],
        out_specs=rows_of,
        out_shape=jax.ShapeDtypeStruct((seq, width), BF),
        compiler_params=room("every_query"),
        cost_estimate=cost(COSTS["every_query"]),
        name="every_query",
    )(after(normed_near, second_parts[0]), normed_far, full_qkv, cos, sin)
    come_y = after(come_y, every_query)
    come_cy = links.swap(come_y, near_sides)
    sent = second.step(come_y)
    first_low, first_high = pl.pallas_call(
        middle_grad_kernel,
        in_specs=[pl.BlockSpec(memory_space=pltpu.SMEM)] + [vm] * 5,
        out_specs=[vm] * 2,
        out_shape=[jax.ShapeDtypeStruct((CHUNKS // 2, 16, length), BF)] * 2,
        scratch_shapes=[
            pltpu.VMEM((part, n_dp * own), BF),
            pltpu.VMEM((n_dp * own, 5 * width), BF),
            pltpu.VMEM((rows, 3 * width), F32),
            pltpu.VMEM((rows, width), F32),
            pltpu.VMEM((frows, width), F32),
        ],
        compiler_params=room("middle_grad"),
        cost_estimate=cost(COSTS["middle_grad"]),
        name="middle_grad",
    )(svec, after(share_mine, sent), share_core, come_c, come_y, come_cy)
    first = Chain(links, FIRST_WALKS, first_low, first_high)
    gathered = links.swap(payload, links.both(links.bits - 1))
    gathered = jnp.concatenate([payload, after(gathered, first_high)], axis=0)
    late = first.step(second.step(first.step(second.step(gathered))))
    for i in reversed(range(1, links.bits - 1)):
        come = links.swap(gathered, links.both(i))
        gathered = jnp.concatenate([gathered, after(come, late)], axis=0)
    gathered_far = links.swap(gathered, links.both(0))
    late = second.step(first.step(gathered))

    d_key, d_value = pl.pallas_call(
        attend_keys_kernel,
        grid=(groups,),
        in_specs=[
            seq_pair, own_pair, own_pair,
            pl.BlockSpec((n_ctx // 2, own + 16, 128), lambda g: (0, 0, g)),
            pl.BlockSpec((n_ctx // 2, own + 16, 128), lambda g: (0, 0, g)),
            whole((own, 128)), whole((own, 128)),
        ],
        out_specs=[own_pair, own_pair],
        out_shape=[jax.ShapeDtypeStruct((own, width), BF)] * 2,
        compiler_params=room("attend_keys"),
        cost_estimate=cost(COSTS["attend_keys"]),
        name="attend_keys",
    )(every_query, keys_near, values_near, gathered, after(gathered_far, late), cos, sin)

    late = second.step(first.step(d_key))

    tokens_grad = pl.pallas_call(
        tokens_grad_kernel,
        in_specs=[vm] * 7,
        out_specs=vm,
        out_shape=jax.ShapeDtypeStruct((own, width), F32),
        compiler_params=room("tokens_grad"),
        cost_estimate=cost(COSTS["tokens_grad"]),
        name="tokens_grad",
    )(after(tokens, late), d_query, d_key, d_value, full_qkv, gains_full, d_mid)
    late = tokens_grad
    while first.more() or second.more():
        for chain in (first, second):
            if chain.more():
                late = chain.step(late)

    def finish(chain, weight, shapes, mark, row, name):
        half = CHUNKS // 2
        done = ()
        for begin, part in ((0, chain.keep), (half, chain.recv)):

            def rows_at(count, cols, begin=begin):
                return pl.BlockSpec((count, cols), lambda i, s: ((i + begin) ^ s[mark], 0))

            big = [jax.ShapeDtypeStruct((r * CHUNKS, c), F32) for r, c in shapes]
            done = pl.pallas_call(
                functools.partial(finish_kernel, shapes=shapes, mark=mark, row=row, begin=begin),
                grid_spec=pltpu.PrefetchScalarGridSpec(
                    num_scalar_prefetch=1,
                    grid=(half,),
                    in_specs=[
                        pl.BlockSpec((1, 16, part.shape[2]), lambda i, s: (i, 0, 0)),
                        rows_at(*shapes[0]),
                        whole((2, rows)),
                    ]
                    + ([whole((1, rows))] + [pl.BlockSpec(memory_space=pl.ANY)] * len(shapes) if begin else []),
                    out_specs=[rows_at(*shape) for shape in shapes] + [whole((1, rows))],
                ),
                out_shape=big + [jax.ShapeDtypeStruct((1, rows), F32)],
                input_output_aliases={5 + i: i for i in range(len(shapes))} if begin else {},
                compiler_params=room(name),
                cost_estimate=cost(COSTS[name]),
                name=name,
            )(svec, part, weight, gains, *((done[-1], *done[:-1]) if begin else ()))
        return done

    first_shapes = ((step, 3 * width), (step, width), (fstep, width))
    in_grad, out_grad, down_grad, gain_mlp_sum = finish(first, w_in, first_shapes, 2, 1, "finish_first")
    qkv_grad, gain_attn_sum = finish(second, w_qkv, ((step, 3 * width),), 3, 0, "finish_second")

    return (
        layer_out,
        tokens_grad,
        qkv_grad,
        out_grad,
        in_grad,
        down_grad,
        gain_attn_sum.reshape(rows),
        gain_mlp_sum.reshape(rows),
    )


def solution(mesh):
    return jax.shard_map(
        functools.partial(on_device, n_dp=mesh.shape["dp"], n_ctx=mesh.shape["ctx"]),
        mesh=mesh,
        in_specs=(
            P(("dp", "ctx"), None),
            P("dp", None),
            P("dp", None),
            P("dp", None),
            P("dp", None),
            P("dp"),
            P("dp"),
            P(("dp", "ctx"), None),
        ),
        out_specs=(
            P(("dp", "ctx"), None),
            P(("dp", "ctx"), None),
            P("dp", None),
            P("dp", None),
            P("dp", None),
            P("dp", None),
            P("dp"),
            P("dp"),
        ),
        check_vma=False,
    )
```
